256 devices in a mesh: front: 16 (over z, core), tile: 16 (over x, y).
Axes of the slice: x: 4, y: 4, z: 8, core: 2. Of those that a mesh axis runs over, the one named last changes fastest.
Arguments:
- child_front: float32 [16, 8192, 1536], P('front', 'tile')
- parent_front: float32 [16, 8192, 512], P('front', 'tile')
- child_map: int32 [16, 60], replicated, may hold values from 1 to 62, as said below
Outputs:
- child_panel: float32 [16, 8192, 512], P('front', 'tile')
- parent_result: float32 [16, 8192, 512], P('front', 'tile')
The draws below stay inside these ranges and needn't reach their ends.
Inputs may be any that keep to these rules, and one draw needn't show every extreme that they name: child_map[f] is strictly increasing: each child's Schur tiles go, in order, to distinct parent tiles; parent tile 0 and the last parent tile receive nothing.
All inputs are finite; a program needn't handle non-finite values.
Results may differ from the reference program's by a relative error of at most 0.00028.
Values sent between devices are 32-bit elements; how exact they have to be, the bound alone decides.
No kernel may reach another device: no remote copies, remote signals or barrier semaphores. Data moves between devices by JAX's collectives and lax.ppermute only.
A program may use at most 64 MiB of HBM per device.

```python
import jax
import jax.numpy as jnp
from jax import lax

ORDER = 8192
TILE_ROWS = 128
PIVOTS = 512
HALF_COLS = 512
FRONTS = 16
SCHUR_TILES = 60


def front_values(key, shape, boost_mask_fn):
    key_base, key_boost = jax.random.split(key, 2)
    base = jax.random.truncated_normal(key_base, -4.0, 4.0, shape, jnp.float32)
    slices = lax.broadcasted_iota(jnp.int32, shape, 0)
    row_ids = lax.broadcasted_iota(jnp.int32, shape, 1)
    col_ids = lax.broadcasted_iota(jnp.int32, shape, 2)
    boost = jax.random.uniform(key_boost, shape[:-1] + (1,), jnp.float32, 80.0, 160.0)
    chosen = (row_ids == col_ids) & (row_ids < PIVOTS) & boost_mask_fn(slices)
    return base + jnp.where(chosen, boost, 0.0)


def draw_child_front(key, part):
    key = jax.random.fold_in(key, 11)
    return front_values(key, (FRONTS, ORDER, PIVOTS + 2 * HALF_COLS), lambda slices: slices >= 0)


def draw_parent_front(key, part):
    key = jax.random.fold_in(key, 12)
    return front_values(key, (FRONTS, ORDER, HALF_COLS), lambda slices: slices % 2 == 1)


def one_child(child_key):
    total = ORDER // TILE_ROWS
    pivot_tiles = PIVOTS // TILE_ROWS
    inner = jax.random.permutation(child_key, total - 4)[:pivot_tiles - 2] + 2
    tile_ids = jnp.arange(total)
    gaps = (tile_ids == 0) | (tile_ids == total - 1) | jnp.any(tile_ids[:, None] == inner[None, :], axis=1)
    order = jnp.argsort(gaps.astype(jnp.int32), stable=True)
    return order[:total - pivot_tiles]


def draw_child_map(key, part):
    key = jax.random.fold_in(key, 13)
    maps_all = jax.vmap(one_child)(jax.random.split(key, FRONTS))
    return maps_all.astype(jnp.int32)


def setup_inputs(seed: int = 0) -> dict:
    arg_keys = jax.random.split(jax.random.key(seed), 4)
    return {
        "child_front": draw_child_front(jax.random.fold_in(arg_keys[3], 71), 0),
        "parent_front": draw_parent_front(jax.random.fold_in(arg_keys[3], 71), 0),
        "child_map": draw_child_map(jax.random.fold_in(arg_keys[3], 71), 0),
    }


def panel_step(window):
    width_all = window.shape[1]
    factor = jnp.linalg.cholesky(window[:PIVOTS, :PIVOTS])
    panel = lax.linalg.triangular_solve(factor, window[:, :PIVOTS], left_side=False, lower=True, transpose_a=True)
    rest = window[:, PIVOTS:] - jnp.dot(panel, panel[PIVOTS:width_all].T, precision=lax.Precision.HIGHEST)
    return (panel, rest)

def reference(child_front, parent_front, child_map):
    panels = []
    results = []
    for parent_idx in range(FRONTS // 2):
        whole_parent = jnp.concatenate([parent_front[2 * parent_idx + 1], parent_front[2 * parent_idx]], axis=1)
        tiles_all = whole_parent.reshape(ORDER // TILE_ROWS, TILE_ROWS, 2 * HALF_COLS)
        for side in range(2):
            child_idx = 2 * parent_idx + side
            panel, rest = panel_step(child_front[child_idx])
            panels.append(panel)
            update = rest[PIVOTS:].reshape(SCHUR_TILES, TILE_ROWS, 2 * HALF_COLS)
            tiles_all = tiles_all.at[child_map[child_idx]].add(update)
        parent_panel, parent_rest = panel_step(tiles_all.reshape(ORDER, 2 * HALF_COLS))
        whole_out = jnp.concatenate([parent_panel, parent_rest], axis=1)
        results.append(whole_out[:, HALF_COLS:])
        results.append(whole_out[:, :HALF_COLS])
    return (jnp.stack(panels), jnp.stack(results))
```

```python
import jax
import jax.numpy as jnp
from jax import lax
from jax.experimental import pallas as pl
from jax.experimental.pallas import tpu as pltpu
from jax.sharding import PartitionSpec as P

B = 128
N = 512
NT = ((1,), (1,))
NN = ((1,), (0,))
F32 = jnp.float32
VMEM = pl.BlockSpec(memory_space=pltpu.VMEM)
SMEM = pl.BlockSpec(memory_space=pltpu.SMEM)
PARAMS = pltpu.CompilerParams(vmem_limit_bytes=48 * 1024 * 1024)


def row_of(v, j):
    return jnp.broadcast_to(v[j : j + 1, :], v.shape)


def column_of(v, j):
    return jnp.broadcast_to(v[:, j : j + 1], (v.shape[0], B))


def inverse_factor(rows_at):
    sub = lax.broadcasted_iota(jnp.int32, (8, B), 0)
    lane = lax.broadcasted_iota(jnp.int32, (8, B), 1)
    left = [rows_at(q) for q in range(16)]
    right = [jnp.where(lane == sub + 8 * q, 1.0, 0.0).astype(F32) for q in range(16)]
    out = []
    for p in range(16):
        cols = [column_of(left[p], 8 * p + j) for j in range(8)]
        v, xv, xf = left[p], right[p], right[p]
        diag = jnp.zeros((8, B), F32)
        for j in range(8):
            pivot = row_of(cols[j], j)
            recip = 1.0 / pivot
            diag = jnp.where(sub == j, pivot, diag)
            scale = jnp.where(sub == j, 0.0, cols[j]) * recip
            below = jnp.where(sub > j, cols[j], 0.0) * recip
            for m in range(j + 1, 8):
                cm = row_of(cols[m], j)
                cols[m] = jnp.where(sub == j, cm * recip, cols[m] - scale * cm)
            vr, xr, fr = row_of(v, j), row_of(xv, j), row_of(xf, j)
            v = jnp.where(sub == j, vr * recip, v - scale * vr)
            xv = jnp.where(sub == j, xr * recip, xv - scale * xr)
            xf = xf - below * fr
        out.append(xf * lax.rsqrt(diag))
        if p < 15:
            w = [row_of(v, j) for j in range(8)]
            xw = [row_of(xv, j) for j in range(8)]
            for q in range(p + 1, 16):
                c = [column_of(left[q], 8 * p + j) for j in range(8)]
                s, x = c[0] * w[0], c[0] * xw[0]
                for j in range(1, 8):
                    s = s + c[j] * w[j]
                    x = x + c[j] * xw[j]
                left[q] = left[q] - s
                right[q] = right[q] - x
    return jnp.concatenate(out, axis=0)


def dot_f32(a, b, dims):
    return lax.dot_general(
        a, b, (dims, ((), ())), precision=lax.Precision.HIGHEST, preferred_element_type=F32
    )


def at(i):
    return pl.ds(pl.multiple_of(i * B, B), B)


def factor_kernel(rows, a_ref, x_ref, s_ref, l_ref):
    l_ref[...] = a_ref[:, :rows, :].reshape(N, N)
    for i in range(4):
        for j in range(i + 1):
            s_ref[i * B : (i + 1) * B, j * B : (j + 1) * B] = 0.5 * (
                l_ref[i * B : (i + 1) * B, j * B : (j + 1) * B]
                + l_ref[j * B : (j + 1) * B, i * B : (i + 1) * B].T
            )
    x_ref[...] = jnp.zeros_like(x_ref)

    def step(k, carry):
        k0 = pl.multiple_of(k * B, B)
        xk = inverse_factor(lambda q: s_ref[pl.ds(pl.multiple_of(k0 + 8 * q, 8), 8), at(k)])
        x_ref[at(k), at(k)] = xk

        def x_row(j, carry):
            def acc(m, t):
                return t + dot_f32(l_ref[at(k), at(m)], x_ref[at(m), at(j)], NN)

            t = lax.fori_loop(j, k, acc, jnp.zeros((B, B), F32))
            x_ref[at(k), at(j)] = -dot_f32(xk, t, NN)
            return carry

        lax.fori_loop(0, k, x_row, 0)

        def l_col(i, carry):
            l_ref[at(i), at(k)] = dot_f32(s_ref[at(i), at(k)], xk, NT)

            def update(j, carry):
                s_ref[at(i), at(j)] -= dot_f32(l_ref[at(i), at(k)], l_ref[at(j), at(k)], NT)
                return carry

            lax.fori_loop(k + 1, i + 1, update, 0)
            return carry

        lax.fori_loop(k + 1, 4, l_col, 0)
        return carry

    lax.fori_loop(0, 4, step, 0)


def inverse_of(block, rows):
    return pl.pallas_call(
        lambda *refs: factor_kernel(rows, *refs),
        out_shape=jax.ShapeDtypeStruct((N, N), F32),
        in_specs=[VMEM],
        out_specs=VMEM,
        scratch_shapes=[pltpu.VMEM((N, N), F32)] * 2,
        compiler_params=PARAMS,
        cost_estimate=pl.CostEstimate(flops=30_000_000_000, bytes_accessed=2**21, transcendentals=0),
    )(block)


def split(x):
    hi = x.astype(jnp.bfloat16)
    return hi, (x - hi.astype(F32)).astype(jnp.bfloat16)


def dot_split(a, b, dims=NT):
    def dot(u, v):
        return lax.dot_general(u, v, (dims, ((), ())), preferred_element_type=F32)

    return dot(a[0], b[0]) + (dot(a[0], b[1]) + dot(a[1], b[0]))


def child_kernel(ids, cmap, a_ref, x_ref, top_ref, panel_ref, keep_ref, send_ref):
    front, tile = ids[0], ids[1]
    parity = lax.rem(front, 2)
    x = split(x_ref[...])
    tops = [split(dot_split(split(top_ref[:, h].reshape(N, N)), x)) for h in range(2)]
    keep_ref[...] = jnp.zeros_like(keep_ref)
    send_ref[...] = jnp.zeros_like(send_ref)
    panel_ref[...] = dot_split(split(a_ref[0, :, :N]), x)
    for i in range(4):
        rows = slice(i * B, (i + 1) * B)
        panel = split(panel_ref[rows, :])
        place = cmap[front, jnp.maximum(4 * tile - 4 + i, 0)] - 4 * (tile - 1)
        first = a_ref[0, rows, N : 2 * N] - dot_split(panel, tops[0])
        second = a_ref[0, rows, 2 * N :] - dot_split(panel, tops[1])

        @pl.when(tile > 0)
        def _():
            keep_ref[at(place), :] = jnp.where(parity == 1, first, second)
            send_ref[at(place), :] = jnp.where(parity == 1, second, first)


def child_step(ids, cmap, front_vals, x, tops):
    return pl.pallas_call(
        child_kernel,
        out_shape=[jax.ShapeDtypeStruct((N, N), F32)] + [jax.ShapeDtypeStruct((2 * N, N), F32)] * 2,
        in_specs=[SMEM, SMEM, VMEM, VMEM, VMEM],
        out_specs=[VMEM] * 3,
        compiler_params=PARAMS,
        cost_estimate=pl.CostEstimate(flops=5_000_000_000, bytes_accessed=2**23, transcendentals=0),
    )(ids, cmap, front_vals, x, tops)


def parent_kernel(ids, own_ref, other_ref, x_ref, mine_ref, theirs_ref, out_ref):
    x = split(x_ref[...])
    parity = lax.rem(ids[0], 2)

    @pl.when(parity == 1)
    def _():
        out_ref[...] = dot_split(split(own_ref[...]), x)

    @pl.when(parity == 0)
    def _():
        top = jnp.concatenate([theirs_ref[...], mine_ref[:, 32:, :]], axis=1).reshape(N, N)
        top = split(dot_split(split(top), x))
        panel = split(dot_split(split(other_ref[...]), x))
        out_ref[...] = own_ref[...] - dot_split(panel, top)


def parent_step(ids, own, other, x, mine, theirs):
    return pl.pallas_call(
        parent_kernel,
        out_shape=jax.ShapeDtypeStruct((N, N), F32),
        in_specs=[SMEM] + [VMEM] * 5,
        out_specs=VMEM,
        compiler_params=PARAMS,
        cost_estimate=pl.CostEstimate(flops=5_000_000_000, bytes_accessed=2**23, transcendentals=0),
    )(ids, own, other, x, mine, theirs)


def scattered(x):
    return lax.all_to_all(x.reshape(16, 32, N), "tile", 0, 0)


def gathered(piece):
    return lax.all_to_all(jnp.broadcast_to(piece[None], (16,) + piece.shape), "tile", 0, 0)


def sibling(x):
    return lax.ppermute(x, "front", [(i, i ^ 1) for i in range(16)])


def local(child_front, parent_front, child_map):
    tile = lax.axis_index("tile")
    front = lax.axis_index("front")
    odd = front % 2 == 1
    ids = jnp.stack([front, tile]).astype(jnp.int32)
    parent_vals = parent_front[0]
    pivots_ahead = lax.ppermute(parent_vals, "tile", [(0, 1)])

    pieces = scattered(child_front[0, :, :N])
    tops = lax.all_gather(pieces[1:3], "tile")
    child_x = inverse_of(gathered(pieces[0]), 32)
    child_panel, keep, send = child_step(ids, child_map, child_front, child_x, tops)

    placed = keep + sibling(send)
    lower = placed[:N]
    upper = placed[N:] + parent_vals
    arrived = lax.ppermute(lower, "tile", [(i, i - 1) for i in range(1, 16)])
    outgoing = jnp.where(odd, lower + pivots_ahead, sibling(upper))
    parts = scattered(outgoing)
    mine = parts[1:3]
    theirs = sibling(mine)
    pivot_piece = jnp.where(odd, mine[0], theirs[0])
    top_piece = jnp.where(odd, mine[1] + theirs[0], theirs[1] + mine[0])
    top_half = jnp.where(odd, top_piece[:16], top_piece[16:])
    whole = gathered(jnp.concatenate([pivot_piece, top_half], axis=0))
    top_theirs = sibling(whole[:, 32:, :])
    assembled = upper + arrived
    other = sibling(assembled)
    parent_x = inverse_of(whole, 32)
    result = parent_step(ids, assembled, other, parent_x, whole, top_theirs)
    return (child_panel[None], result[None])


def solution(mesh):
    return jax.shard_map(
        local,
        mesh=mesh,
        in_specs=(P("front", "tile", None), P("front", "tile", None), P()),
        out_specs=(P("front", "tile", None), P("front", "tile", None)),
        check_vma=False,
    )
```

```python
import jax
import jax.numpy as jnp
from jax import lax
from jax.experimental import pallas as pl
from jax.experimental.pallas import tpu as pltpu
from jax.sharding import PartitionSpec as P

B = 128
N = 512
NT = ((1,), (1,))
NN = ((1,), (0,))
F32 = jnp.float32
VMEM = pl.BlockSpec(memory_space=pltpu.VMEM)
SMEM = pl.BlockSpec(memory_space=pltpu.SMEM)
PARAMS = pltpu.CompilerParams(vmem_limit_bytes=48 * 1024 * 1024)


def row_of(v, j):
    return jnp.broadcast_to(v[j : j + 1, :], v.shape)


def column_of(v, j):
    return jnp.broadcast_to(v[:, j : j + 1], (v.shape[0], B))


def inverse_factor(rows_at):
    sub = lax.broadcasted_iota(jnp.int32, (8, B), 0)
    lane = lax.broadcasted_iota(jnp.int32, (8, B), 1)
    left = [rows_at(q) for q in range(16)]
    right = [jnp.where(lane == sub + 8 * q, 1.0, 0.0).astype(F32) for q in range(16)]
    out = []
    for p in range(16):
        cols = [column_of(left[p], 8 * p + j) for j in range(8)]
        v, xv, xf = left[p], right[p], right[p]
        diag = jnp.zeros((8, B), F32)
        for j in range(8):
            pivot = row_of(cols[j], j)
            recip = 1.0 / pivot
            diag = jnp.where(sub == j, pivot, diag)
            scale = jnp.where(sub == j, 0.0, cols[j]) * recip
            below = jnp.where(sub > j, cols[j], 0.0) * recip
            for m in range(j + 1, 8):
                cm = row_of(cols[m], j)
                cols[m] = jnp.where(sub == j, cm * recip, cols[m] - scale * cm)
            vr, xr, fr = row_of(v, j), row_of(xv, j), row_of(xf, j)
            v = jnp.where(sub == j, vr * recip, v - scale * vr)
            xv = jnp.where(sub == j, xr * recip, xv - scale * xr)
            xf = xf - below * fr
        out.append(xf * lax.rsqrt(diag))
        if p < 15:
            w = [row_of(v, j) for j in range(8)]
            xw = [row_of(xv, j) for j in range(8)]
            for q in range(p + 1, 16):
                c = [column_of(left[q], 8 * p + j) for j in range(8)]
                s, x = c[0] * w[0], c[0] * xw[0]
                for j in range(1, 8):
                    s = s + c[j] * w[j]
                    x = x + c[j] * xw[j]
                left[q] = left[q] - s
                right[q] = right[q] - x
    return jnp.concatenate(out, axis=0)


def dot_f32(a, b, dims):
    return lax.dot_general(
        a, b, (dims, ((), ())), precision=lax.Precision.HIGHEST, preferred_element_type=F32
    )


def at(i):
    return pl.ds(pl.multiple_of(i * B, B), B)


LOWER = [(i, j) for i in range(4) for j in range(i + 1)]


def eliminate(steps, s_ref, l_ref, x_ref):
    def step(k, carry):
        k0 = pl.multiple_of(k * B, B)
        xk = inverse_factor(lambda q: s_ref[pl.ds(pl.multiple_of(k0 + 8 * q, 8), 8), at(k)])
        x_ref[at(k), at(k)] = xk

        def x_row(j, carry):
            def acc(m, t):
                return t + dot_f32(l_ref[at(k), at(m)], x_ref[at(m), at(j)], NN)

            t = lax.fori_loop(j, k, acc, jnp.zeros((B, B), F32))
            x_ref[at(k), at(j)] = -dot_f32(xk, t, NN)
            return carry

        lax.fori_loop(0, k, x_row, 0)

        def l_col(i, carry):
            l_ref[at(i), at(k)] = dot_f32(s_ref[at(i), at(k)], xk, NT)

            def update(j, carry):
                s_ref[at(i), at(j)] -= dot_f32(l_ref[at(i), at(k)], l_ref[at(j), at(k)], NT)
                return carry

            lax.fori_loop(k + 1, i + 1, update, 0)
            return carry

        lax.fori_loop(k + 1, 4, l_col, 0)
        return carry

    lax.fori_loop(steps[0], steps[1], step, 0)


def unpack(packed, s_ref):
    for b, (i, j) in enumerate(LOWER):
        s_ref[i * B : (i + 1) * B, j * B : (j + 1) * B] = packed[b * B : (b + 1) * B, :]


def whole_kernel(a_ref, x_ref, s_ref, l_ref):
    unpack(a_ref[...].reshape(1280, B), s_ref)
    x_ref[...] = jnp.zeros_like(x_ref)
    eliminate((0, 4), s_ref, l_ref, x_ref)


def first_kernel(ids, mine_ref, theirs_ref, x_ref, s_ref, l_ref, p_ref):
    parity = lax.rem(ids[0], 2)
    p_ref[pl.ds(pl.multiple_of((1 - parity) * 640, 640), 640), :] = mine_ref[:, :40, :].reshape(640, B)
    p_ref[pl.ds(pl.multiple_of(parity * 640, 640), 640), :] = theirs_ref[...].reshape(640, B)
    unpack(p_ref, s_ref)
    x_ref[...] = jnp.zeros_like(x_ref)
    eliminate((0, 3), s_ref, l_ref, x_ref)


def last_kernel(xin_ref, s_ref, l_ref, x_ref):
    x_ref[...] = xin_ref[...]
    eliminate((3, 4), s_ref, l_ref, x_ref)


SQUARE = jax.ShapeDtypeStruct((N, N), F32)


def cost(gflop):
    return pl.CostEstimate(flops=int(gflop * 1e9), bytes_accessed=2**21, transcendentals=0)


def inverse_whole(packed):
    return pl.pallas_call(
        whole_kernel,
        out_shape=SQUARE,
        in_specs=[VMEM],
        out_specs=VMEM,
        scratch_shapes=[pltpu.VMEM((N, N), F32)] * 2,
        compiler_params=PARAMS,
        cost_estimate=cost(25),
    )(packed)


def inverse_first(ids, mine, theirs):
    return pl.pallas_call(
        first_kernel,
        out_shape=[SQUARE] * 3,
        in_specs=[SMEM, VMEM, VMEM],
        out_specs=[VMEM] * 3,
        scratch_shapes=[pltpu.VMEM((1280, B), F32)],
        compiler_params=PARAMS,
        cost_estimate=cost(20),
    )(ids, mine, theirs)


def inverse_last(x, s, l):
    return pl.pallas_call(
        last_kernel,
        out_shape=SQUARE,
        in_specs=[VMEM] * 3,
        out_specs=VMEM,
        compiler_params=PARAMS,
        cost_estimate=cost(6),
    )(x, s, l)


def split(x):
    hi = x.astype(jnp.bfloat16)
    return hi, (x - hi.astype(F32)).astype(jnp.bfloat16)


def dot_split(a, b, dims=NT):
    def dot(u, v):
        return lax.dot_general(u, v, (dims, ((), ())), preferred_element_type=F32)

    return dot(a[0], b[0]) + (dot(a[0], b[1]) + dot(a[1], b[0]))


def symmetric(ref, i, j):
    return 0.5 * (
        ref[i * B : (i + 1) * B, j * B : (j + 1) * B]
        + ref[j * B : (j + 1) * B, i * B : (i + 1) * B].T
    )


def spread_kernel(ids, a_ref, out_ref, p_ref):
    @pl.when(ids[1] > 0)
    def _():
        for c in range(4):
            out_ref[:, 32 * c : 32 * c + 32, :] = a_ref[0, :, c * B : (c + 1) * B].reshape(16, 32, B)

    @pl.when(ids[1] == 0)
    def _():
        for b, (i, j) in enumerate(LOWER):
            p_ref[b * B : (b + 1) * B, :] = symmetric(a_ref.at[0], i, j)
        out_ref[:, :80, :] = p_ref[...].reshape(16, 80, B)
        out_ref[:, 80:, :] = jnp.zeros((16, 48, B), F32)


def spread(ids, front_vals):
    return pl.pallas_call(
        spread_kernel,
        grid=(1,),
        out_shape=jax.ShapeDtypeStruct((16, B, B), F32),
        in_specs=[SMEM, pl.BlockSpec((1, N, N), lambda i: (0, 0, 0))],
        out_specs=pl.BlockSpec((16, B, B), lambda i: (0, 0, 0)),
        scratch_shapes=[pltpu.VMEM((1280, B), F32)],
        compiler_params=PARAMS,
    )(ids, front_vals)


def place_of(cmap, front, tile, i):
    return cmap[front, jnp.maximum(4 * tile - 4 + i, 0)] - 4 * (tile - 1)


def corner_kernel(
    ids, cmap, a_ref, ahead_ref, x_ref, pp_ref, pf_ref, panel_ref, keep_ref, send_ref, b_ref, p_ref
):
    front, tile = ids[0], ids[1]
    parity = lax.rem(front, 2)
    x = split(x_ref[...])
    panel_ref[...] = dot_split(split(a_ref[0, :, :N]), x)
    top = split(dot_split(split(jnp.where(tile == 1, a_ref[0, :, :N], ahead_ref[...])), x))
    b_ref[...] = jnp.zeros_like(b_ref)
    for i in range(4):
        rows = slice(i * B, (i + 1) * B)
        first = a_ref[0, rows, N:] - dot_split(split(panel_ref[rows, :]), top)

        @pl.when(tile > 0)
        def _():
            b_ref[at(place_of(cmap, front, tile, i)), :] = first

    @pl.when((tile == 1) & (parity == 1))
    def _():
        b_ref[:N, :] += pp_ref[...]
        b_ref[N:, :] += pf_ref[...]

    for b, (i, j) in enumerate(LOWER):
        p_ref[b * B : (b + 1) * B, :] = symmetric(b_ref, i, j)
    base = jnp.where(tile == 1, N, 0)
    for ref, half in ((keep_ref, 1 - parity), (send_ref, parity)):
        ref[:, :40, :] = p_ref[pl.ds(pl.multiple_of(half * 640, 640), 640), :].reshape(16, 40, B)
        rows = pl.ds(pl.multiple_of(base + half * 256, 256), 256)
        for c in range(4):
            ref[:, 40 + 16 * c : 56 + 16 * c, :] = b_ref[rows, c * B : (c + 1) * B].reshape(16, 16, B)


def corner(ids, cmap, front_vals, ahead, x, pp, pf):
    full = pl.BlockSpec((N, N), lambda i: (0, 0))
    piece = pl.BlockSpec((16, 104, B), lambda i: (0, 0, 0))
    return pl.pallas_call(
        corner_kernel,
        grid=(1,),
        out_shape=[SQUARE] + [jax.ShapeDtypeStruct((16, 104, B), F32)] * 2,
        in_specs=[SMEM, SMEM, pl.BlockSpec((1, N, 2 * N), lambda i: (0, 0, 0)), full, full, full, full],
        out_specs=[full, piece, piece],
        scratch_shapes=[pltpu.VMEM((2 * N, N), F32), pltpu.VMEM((1280, B), F32)],
        compiler_params=PARAMS,
        cost_estimate=cost(3),
    )(ids, cmap, front_vals, ahead, x, pp, pf)


def schur_kernel(ids, cmap, a_ref, panel_ref, x_ref, top_ref, keep_ref, send_ref):
    front, tile = ids[0], ids[1]
    parity = lax.rem(front, 2)
    x = split(x_ref[...])
    tops = []
    for h in range(2):
        raw = [top_ref[:, h, 32 * c : 32 * c + 32, :].reshape(N, B) for c in range(4)]
        tops.append(split(dot_split(split(jnp.concatenate(raw, axis=1)), x)))
    keep_ref[...] = jnp.zeros_like(keep_ref)
    send_ref[...] = jnp.zeros_like(send_ref)
    for i in range(4):
        rows = slice(i * B, (i + 1) * B)
        panel = split(panel_ref[rows, :])
        place = place_of(cmap, front, tile, i)
        first = a_ref[0, rows, N : 2 * N] - dot_split(panel, tops[0])
        second = a_ref[0, rows, 2 * N :] - dot_split(panel, tops[1])

        @pl.when(tile > 0)
        def _():
            keep_ref[at(place), :] = jnp.where(parity == 1, first, second)
            send_ref[at(place), :] = jnp.where(parity == 1, second, first)


def schur(ids, cmap, front_vals, panel, x, tops):
    return pl.pallas_call(
        schur_kernel,
        out_shape=[jax.ShapeDtypeStruct((2 * N, N), F32)] * 2,
        in_specs=[SMEM, SMEM, VMEM, VMEM, VMEM, VMEM],
        out_specs=[VMEM] * 2,
        compiler_params=PARAMS,
        cost_estimate=cost(8),
    )(ids, cmap, front_vals, panel, x, tops)


def parent_kernel(ids, own_ref, other_ref, x_ref, mine_ref, theirs_ref, out_ref):
    x = split(x_ref[...])
    parity = lax.rem(ids[0], 2)

    @pl.when(parity == 1)
    def _():
        out_ref[...] = dot_split(split(own_ref[...]), x)

    @pl.when(parity == 0)
    def _():
        top = [
            jnp.concatenate(
                [
                    theirs_ref[:, 16 * c : 16 * c + 16, :].reshape(256, B),
                    mine_ref[:, 40 + 16 * c : 56 + 16 * c, :].reshape(256, B),
                ],
                axis=0,
            )
            for c in range(4)
        ]
        top = split(dot_split(split(jnp.concatenate(top, axis=1)), x))
        panel = split(dot_split(split(other_ref[...]), x))
        out_ref[...] = own_ref[...] - dot_split(panel, top)


def parent_step(ids, own, other, x, mine, theirs):
    return pl.pallas_call(
        parent_kernel,
        out_shape=SQUARE,
        in_specs=[SMEM] + [VMEM] * 5,
        out_specs=VMEM,
        compiler_params=PARAMS,
        cost_estimate=cost(4),
    )(ids, own, other, x, mine, theirs)


def exchanged(x):
    return lax.all_to_all(x, "tile", 0, 0)


def gathered(piece):
    return exchanged(jnp.broadcast_to(piece[None], (16,) + piece.shape))


def sibling(x):
    return lax.ppermute(x, "front", [(i, i ^ 1) for i in range(16)])


def local(child_front, parent_front, child_map):
    tile = lax.axis_index("tile")
    front = lax.axis_index("front")
    ids = jnp.stack([front, tile]).astype(jnp.int32)
    parent_vals = parent_front[0]

    pieces = exchanged(spread(ids, child_front))
    tops = lax.all_gather(pieces[1:3], "tile")
    pivot = gathered(pieces[0, :80])
    columns, parents, pivot = lax.optimization_barrier((child_front[0, :, :N], parent_vals, pivot))
    ahead = lax.ppermute(columns, "tile", [(1, 2)])
    pivots_ahead = lax.ppermute(
        parents, ("front", "tile"), [(f * 16, f * 16 + 1) for f in range(1, 16, 2)]
    )
    child_x = inverse_whole(pivot)
    child_panel, keep, send = corner(
        ids, child_map, child_front, ahead, child_x, pivots_ahead, parent_vals
    )
    parts = exchanged(keep + sibling(send))
    piece = jnp.concatenate([parts[1, :40], parts[1, 40:] + parts[2, 40:]], axis=0)
    mine = gathered(piece)
    panel_later, _ = lax.optimization_barrier((child_panel, piece))
    keep, send = schur(ids, child_map, child_front, panel_later, child_x, tops)
    theirs = sibling(mine[:, :40])
    top_theirs = sibling(mine[:, 40:])
    own = keep + sibling(send)
    arrived = lax.ppermute(own[:N], "tile", [(i, i - 1) for i in range(1, 16)])
    x, s, l = inverse_first(ids, mine, theirs)
    assembled, _ = lax.optimization_barrier((own[N:] + parent_vals + arrived, x))
    other = sibling(assembled)
    parent_x = inverse_last(x, s, l)
    result = parent_step(ids, assembled, other, parent_x, mine, top_theirs)
    return (child_panel[None], result[None])


def solution(mesh):
    return jax.shard_map(
        local,
        mesh=mesh,
        in_specs=(P("front", "tile", None), P("front", "tile", None), P()),
        out_specs=(P("front", "tile", None), P("front", "tile", None)),
        check_vma=False,
    )
```

```python
import jax
import jax.numpy as jnp
from jax import lax
from jax.experimental import pallas as pl
from jax.experimental.pallas import tpu as pltpu
from jax.sharding import PartitionSpec as P

B = 128
N = 512
NT = ((1,), (1,))
NN = ((1,), (0,))
F32 = jnp.float32
VMEM = pl.BlockSpec(memory_space=pltpu.VMEM)
SMEM = pl.BlockSpec(memory_space=pltpu.SMEM)
PARAMS = pltpu.CompilerParams(vmem_limit_bytes=48 * 1024 * 1024)


def row_of(v, j):
    return jnp.broadcast_to(v[j : j + 1, :], v.shape)


def column_of(v, j):
    return jnp.broadcast_to(v[:, j : j + 1], (v.shape[0], B))


def inverse_factor(rows_at):
    sub = lax.broadcasted_iota(jnp.int32, (8, B), 0)
    lane = lax.broadcasted_iota(jnp.int32, (8, B), 1)
    left = [rows_at(q) for q in range(16)]
    right = [jnp.where(lane == sub + 8 * q, 1.0, 0.0).astype(F32) for q in range(16)]
    out = []
    for p in range(16):
        cols = [column_of(left[p], 8 * p + j) for j in range(8)]
        v, xv = left[p], right[p]
        xf = diag = None
        pivot = row_of(cols[0], 0)
        for j in range(8):
            recip = 1.0 / pivot
            hit = sub == j
            diag = pivot if diag is None else jnp.where(hit, pivot, diag)
            rows = [row_of(cols[m], j) for m in range(j + 1, 8)]
            if j < 7:
                pivot = row_of(cols[j + 1], j + 1) - (rows[0] * rows[0]) * recip
            scale = jnp.where(hit, 0.0, cols[j]) * recip
            for m, cm in zip(range(j + 1, 8), rows):
                cols[m] = jnp.where(hit, cm * recip, cols[m] - scale * cm)
            vr, xr = row_of(v, j), row_of(xv, j)
            xf = xr if xf is None else jnp.where(hit, xr, xf)
            v = jnp.where(hit, vr * recip, v - scale * vr)
            xv = jnp.where(hit, xr * recip, xv - scale * xr)
        out.append(xf * lax.rsqrt(diag))
        if p < 15:
            w = [row_of(v, j) for j in range(8)]
            xw = [row_of(xv, j) for j in range(8)]
            for q in range(p + 1, 16):
                c = [column_of(left[q], 8 * p + j) for j in range(8)]
                left[q] = left[q] - total([c[j] * w[j] for j in range(8)])
                right[q] = right[q] - total([c[j] * xw[j] for j in range(8)])
    return jnp.concatenate(out, axis=0)


def total(terms):
    while len(terms) > 1:
        terms = [terms[i] + terms[i + 1] for i in range(0, len(terms), 2)]
    return terms[0]


def at(i):
    return pl.ds(pl.multiple_of(i * B, B), B)


LOWER = [(i, j) for i in range(4) for j in range(i + 1)]


def eliminate(steps, s_ref, l_ref, x_ref):
    def step(k, carry):
        k0 = pl.multiple_of(k * B, B)
        xk = inverse_factor(lambda q: s_ref[pl.ds(pl.multiple_of(k0 + 8 * q, 8), 8), at(k)])
        x_ref[at(k), at(k)] = xk
        xs = split(xk)
        for c in range(*steps):

            @pl.when(k == c)
            def _():
                lo, hi = c * B, (c + 1) * B
                if c > 0:
                    w = dot_split(split(l_ref[lo:hi, :lo]), split(x_ref[:lo, :lo]), NN)
                    x_ref[lo:hi, :lo] = -dot_split(xs, split(w), NN)
                if c < 3:
                    col = dot_split(split(s_ref[hi:, lo:hi]), xs)
                    l_ref[hi:, lo:hi] = col
                    col = split(col)
                    s_ref[hi:, hi:] -= dot_split(col, col)

        return carry

    lax.fori_loop(steps[0], steps[1], step, 0)


def unpack(packed, s_ref):
    for b, (i, j) in enumerate(LOWER):
        s_ref[i * B : (i + 1) * B, j * B : (j + 1) * B] = packed[b * B : (b + 1) * B, :]


def whole_kernel(a_ref, x_ref, s_ref, l_ref):
    unpack(a_ref[...].reshape(1280, B), s_ref)
    x_ref[...] = jnp.zeros_like(x_ref)
    eliminate((0, 4), s_ref, l_ref, x_ref)


def first_kernel(ids, mine_ref, theirs_ref, x_ref, s_ref, l_ref, p_ref):
    parity = lax.rem(ids[0], 2)
    p_ref[pl.ds(pl.multiple_of((1 - parity) * 640, 640), 640), :] = mine_ref[:, :40, :].reshape(640, B)
    p_ref[pl.ds(pl.multiple_of(parity * 640, 640), 640), :] = theirs_ref[...].reshape(640, B)
    unpack(p_ref, s_ref)
    x_ref[...] = jnp.zeros_like(x_ref)
    eliminate((0, 3), s_ref, l_ref, x_ref)


def last_kernel(xin_ref, s_ref, l_ref, x_ref):
    x_ref[...] = xin_ref[...]
    eliminate((3, 4), s_ref, l_ref, x_ref)


SQUARE = jax.ShapeDtypeStruct((N, N), F32)


def cost(gflop):
    return pl.CostEstimate(flops=int(gflop * 1e9), bytes_accessed=2**21, transcendentals=0)


def inverse_whole(packed):
    return pl.pallas_call(
        whole_kernel,
        out_shape=SQUARE,
        in_specs=[VMEM],
        out_specs=VMEM,
        scratch_shapes=[pltpu.VMEM((N, N), F32)] * 2,
        compiler_params=PARAMS,
        cost_estimate=cost(25),
    )(packed)


def inverse_first(ids, mine, theirs):
    return pl.pallas_call(
        first_kernel,
        out_shape=[SQUARE] * 3,
        in_specs=[SMEM, VMEM, VMEM],
        out_specs=[VMEM] * 3,
        scratch_shapes=[pltpu.VMEM((1280, B), F32)],
        compiler_params=PARAMS,
        cost_estimate=cost(20),
    )(ids, mine, theirs)


def inverse_last(x, s, l):
    return pl.pallas_call(
        last_kernel,
        out_shape=SQUARE,
        in_specs=[VMEM] * 3,
        out_specs=VMEM,
        compiler_params=PARAMS,
        cost_estimate=cost(6),
    )(x, s, l)


def split(x):
    hi = x.astype(jnp.bfloat16)
    return hi, (x - hi.astype(F32)).astype(jnp.bfloat16)


def dot_split(a, b, dims=NT):
    def dot(u, v):
        return lax.dot_general(u, v, (dims, ((), ())), preferred_element_type=F32)

    return dot(a[0], b[0]) + (dot(a[0], b[1]) + dot(a[1], b[0]))


def symmetric(ref, i, j):
    return 0.5 * (
        ref[i * B : (i + 1) * B, j * B : (j + 1) * B]
        + ref[j * B : (j + 1) * B, i * B : (i + 1) * B].T
    )


def spread_kernel(ids, a_ref, out_ref, p_ref):
    @pl.when(ids[1] > 0)
    def _():
        for c in range(4):
            out_ref[:, 32 * c : 32 * c + 32, :] = a_ref[0, :, c * B : (c + 1) * B].reshape(16, 32, B)

    @pl.when(ids[1] == 0)
    def _():
        for b, (i, j) in enumerate(LOWER):
            p_ref[b * B : (b + 1) * B, :] = symmetric(a_ref.at[0], i, j)
        out_ref[:, :80, :] = p_ref[...].reshape(16, 80, B)
        out_ref[:, 80:, :] = jnp.zeros((16, 48, B), F32)


def spread(ids, front_vals):
    return pl.pallas_call(
        spread_kernel,
        grid=(1,),
        out_shape=jax.ShapeDtypeStruct((16, B, B), F32),
        in_specs=[SMEM, pl.BlockSpec((1, N, N), lambda i: (0, 0, 0))],
        out_specs=pl.BlockSpec((16, B, B), lambda i: (0, 0, 0)),
        scratch_shapes=[pltpu.VMEM((1280, B), F32)],
        compiler_params=PARAMS,
    )(ids, front_vals)


def place_of(cmap, front, tile, i):
    return cmap[front, jnp.maximum(4 * tile - 4 + i, 0)] - 4 * (tile - 1)


def corner_kernel(
    ids, cmap, a_ref, ahead_ref, x_ref, pp_ref, pf_ref, panel_ref, keep_ref, send_ref, b_ref, p_ref
):
    front, tile = ids[0], ids[1]
    parity = lax.rem(front, 2)
    x = split(x_ref[...])
    panel_ref[...] = dot_split(split(a_ref[0, :, :N]), x)
    raw = [ahead_ref[:, 32 * c : 32 * c + 32, :].reshape(N, B) for c in range(4)]
    top = split(dot_split(split(jnp.concatenate(raw, axis=1)), x))
    b_ref[...] = jnp.zeros_like(b_ref)
    for i in range(4):
        rows = slice(i * B, (i + 1) * B)
        first = a_ref[0, rows, N:] - dot_split(split(panel_ref[rows, :]), top)

        @pl.when(tile > 0)
        def _():
            b_ref[at(place_of(cmap, front, tile, i)), :] = first

    @pl.when((tile == 1) & (parity == 1))
    def _():
        b_ref[:N, :] += pp_ref[...]
        b_ref[N:, :] += pf_ref[...]

    for b, (i, j) in enumerate(LOWER):
        p_ref[b * B : (b + 1) * B, :] = symmetric(b_ref, i, j)
    base = jnp.where(tile == 1, N, 0)
    for ref, half in ((keep_ref, 1 - parity), (send_ref, parity)):
        ref[:, :40, :] = p_ref[pl.ds(pl.multiple_of(half * 640, 640), 640), :].reshape(16, 40, B)
        rows = pl.ds(pl.multiple_of(base + half * 256, 256), 256)
        for c in range(4):
            ref[:, 40 + 16 * c : 56 + 16 * c, :] = b_ref[rows, c * B : (c + 1) * B].reshape(16, 16, B)


def corner(ids, cmap, front_vals, ahead, x, pp, pf):
    full = pl.BlockSpec((N, N), lambda i: (0, 0))
    piece = pl.BlockSpec((16, 104, B), lambda i: (0, 0, 0))
    lead = pl.BlockSpec((16, B, B), lambda i: (0, 0, 0))
    return pl.pallas_call(
        corner_kernel,
        grid=(1,),
        out_shape=[SQUARE] + [jax.ShapeDtypeStruct((16, 104, B), F32)] * 2,
        in_specs=[SMEM, SMEM, pl.BlockSpec((1, N, 2 * N), lambda i: (0, 0, 0)), lead, full, full, full],
        out_specs=[full, piece, piece],
        scratch_shapes=[pltpu.VMEM((2 * N, N), F32), pltpu.VMEM((1280, B), F32)],
        compiler_params=PARAMS,
        cost_estimate=cost(3),
    )(ids, cmap, front_vals, ahead, x, pp, pf)


def schur_kernel(ids, cmap, a_ref, panel_ref, x_ref, top_ref, keep_ref, send_ref):
    front, tile = ids[0], ids[1]
    parity = lax.rem(front, 2)
    x = split(x_ref[...])
    tops = []
    for h in range(2):
        raw = [
            top_ref[:, h * B + 32 * c : h * B + 32 * c + 32, :].reshape(N, B) for c in range(4)
        ]
        tops.append(split(dot_split(split(jnp.concatenate(raw, axis=1)), x)))
    keep_ref[...] = jnp.zeros_like(keep_ref)
    send_ref[...] = jnp.zeros_like(send_ref)
    for i in range(4):
        rows = slice(i * B, (i + 1) * B)
        panel = split(panel_ref[rows, :])
        place = place_of(cmap, front, tile, i)
        first = a_ref[0, rows, N : 2 * N] - dot_split(panel, tops[0])
        second = a_ref[0, rows, 2 * N :] - dot_split(panel, tops[1])

        @pl.when(tile > 0)
        def _():
            keep_ref[at(place - 1), :] = jnp.where(parity == 1, first, second)
            send_ref[at(place - 1), :] = jnp.where(parity == 1, second, first)


def schur(ids, cmap, front_vals, panel, x, tops):
    return pl.pallas_call(
        schur_kernel,
        out_shape=[jax.ShapeDtypeStruct((6 * B, N), F32)] * 2,
        in_specs=[SMEM, SMEM, VMEM, VMEM, VMEM, VMEM],
        out_specs=[VMEM] * 2,
        compiler_params=PARAMS,
        cost_estimate=cost(8),
    )(ids, cmap, front_vals, panel, x, tops)


def parent_kernel(ids, own_ref, other_ref, x_ref, mine_ref, theirs_ref, out_ref):
    x = split(x_ref[...])
    parity = lax.rem(ids[0], 2)

    @pl.when(parity == 1)
    def _():
        out_ref[...] = dot_split(split(own_ref[...]), x)

    @pl.when(parity == 0)
    def _():
        top = [
            jnp.concatenate(
                [
                    theirs_ref[:, 16 * c : 16 * c + 16, :].reshape(256, B),
                    mine_ref[:, 40 + 16 * c : 56 + 16 * c, :].reshape(256, B),
                ],
                axis=0,
            )
            for c in range(4)
        ]
        top = split(dot_split(split(jnp.concatenate(top, axis=1)), x))
        panel = split(dot_split(split(other_ref[...]), x))
        out_ref[...] = own_ref[...] - dot_split(panel, top)


def parent_step(ids, own, other, x, mine, theirs):
    return pl.pallas_call(
        parent_kernel,
        out_shape=SQUARE,
        in_specs=[SMEM] + [VMEM] * 5,
        out_specs=VMEM,
        compiler_params=PARAMS,
        cost_estimate=cost(4),
    )(ids, own, other, x, mine, theirs)


def fan_tops_kernel(parts_ref, out_ref, sems):
    copies = []
    for t in range(16):
        copies.append(
            pltpu.make_async_copy(parts_ref.at[pl.ds(1, 2)], out_ref.at[t], sems.at[t])
        )
    for copy in copies:
        copy.start()
    for copy in copies:
        copy.wait()


def fan_corner_kernel(parts_ref, out_ref, piece_ref, sems):
    piece_ref[:40, :] = parts_ref[1, :40, :]
    piece_ref[40:, :] = parts_ref[1, 40:, :] + parts_ref[2, 40:, :]
    copies = []
    for t in range(16):
        copies.append(pltpu.make_async_copy(piece_ref, out_ref.at[t], sems.at[t]))
    for copy in copies:
        copy.start()
    for copy in copies:
        copy.wait()


def fanned(kernel, parts, shape, scratch):
    return pl.pallas_call(
        kernel,
        out_shape=pltpu.HBM(shape, F32),
        in_specs=[VMEM],
        out_specs=pl.BlockSpec(memory_space=pltpu.HBM),
        scratch_shapes=scratch + [pltpu.SemaphoreType.DMA((16,))],
        compiler_params=PARAMS,
    )(parts)


def exchanged(x):
    return lax.all_to_all(x, "tile", 0, 0)


def gathered(piece):
    return exchanged(jnp.broadcast_to(piece[None], (16,) + piece.shape))


def sibling(x):
    return lax.ppermute(x, "front", [(i, i ^ 1) for i in range(16)])


def local(child_front, parent_front, child_map):
    tile = lax.axis_index("tile")
    front = lax.axis_index("front")
    ids = jnp.stack([front, tile]).astype(jnp.int32)
    parent_vals = parent_front[0]

    pieces = exchanged(spread(ids, child_front))
    pivot = gathered(pieces[0, :80])
    parents, pieces, pivot = lax.optimization_barrier((parent_vals, pieces, pivot))
    pivots_ahead = lax.ppermute(
        parents, ("front", "tile"), [(f * 16, f * 16 + 1) for f in range(1, 16, 2)]
    )
    fan = fanned(fan_tops_kernel, pieces, (16, 2, B, B), [])
    fan, pivot = lax.optimization_barrier((fan, pivot))
    tops = exchanged(fan).reshape(16, 2 * B, B)
    child_x = inverse_whole(pivot)
    child_panel, keep, send = corner(
        ids, child_map, child_front, tops, child_x, pivots_ahead, parent_vals
    )
    parts = exchanged(keep + sibling(send))
    fan = fanned(fan_corner_kernel, parts, (16, 104, B), [pltpu.VMEM((104, B), F32)])
    fan, panel_later = lax.optimization_barrier((fan, child_panel))
    mine = exchanged(fan)
    keep, send = schur(ids, child_map, child_front, panel_later, child_x, tops)
    send, mine = lax.optimization_barrier((send, mine))
    theirs = sibling(mine[:, :40])
    own = keep + sibling(send)
    top_theirs = sibling(mine[:, 40:])
    arrived = lax.ppermute(own[: 3 * B], "tile", [(i, i - 1) for i in range(1, 16)])
    x, s, l = inverse_first(ids, mine, theirs)
    assembled = (
        parent_vals + jnp.pad(own[3 * B :], ((0, B), (0, 0))) + jnp.pad(arrived, ((B, 0), (0, 0)))
    )
    assembled, _ = lax.optimization_barrier((assembled, x))
    other = sibling(assembled)
    parent_x = inverse_last(x, s, l)
    result = parent_step(ids, assembled, other, parent_x, mine, top_theirs)
    return (child_panel[None], result[None])


def solution(mesh):
    return jax.shard_map(
        local,
        mesh=mesh,
        in_specs=(P("front", "tile", None), P("front", "tile", None), P()),
        out_specs=(P("front", "tile", None), P("front", "tile", None)),
        check_vma=False,
    )
```

```python
import jax
import jax.numpy as jnp
from jax import lax
from jax.experimental import pallas as pl
from jax.experimental.pallas import tpu as pltpu
from jax.sharding import PartitionSpec as P

B = 128
N = 512
NT = ((1,), (1,))
NN = ((1,), (0,))
F32 = jnp.float32
VMEM = pl.BlockSpec(memory_space=pltpu.VMEM)
SMEM = pl.BlockSpec(memory_space=pltpu.SMEM)
PARAMS = pltpu.CompilerParams(vmem_limit_bytes=40 * 1024 * 1024)


def row_of(v, j):
    return jnp.broadcast_to(v[j : j + 1, :], v.shape)


def column_of(v, j):
    return jnp.broadcast_to(v[:, j : j + 1], (v.shape[0], B))


def inverse_factor(rows_at):
    sub = lax.broadcasted_iota(jnp.int32, (8, B), 0)
    lane = lax.broadcasted_iota(jnp.int32, (8, B), 1)
    left = [rows_at(q) for q in range(16)]
    right = [jnp.where(lane == sub + 8 * q, 1.0, 0.0).astype(F32) for q in range(16)]
    out = []
    for p in range(16):
        cols = [column_of(left[p], 8 * p + j) for j in range(8)]
        v, xv = left[p], right[p]
        xf = diag = None
        pivot = row_of(cols[0], 0)
        for j in range(8):
            recip = 1.0 / pivot
            hit = sub == j
            diag = pivot if diag is None else jnp.where(hit, pivot, diag)
            rows = [row_of(cols[m], j) for m in range(j + 1, 8)]
            if j < 7:
                pivot = row_of(cols[j + 1], j + 1) - (rows[0] * rows[0]) * recip
            scale = jnp.where(hit, 0.0, cols[j]) * recip
            for m, cm in zip(range(j + 1, 8), rows):
                cols[m] = jnp.where(hit, cm * recip, cols[m] - scale * cm)
            vr, xr = row_of(v, j), row_of(xv, j)
            xf = xr if xf is None else jnp.where(hit, xr, xf)
            v = jnp.where(hit, vr * recip, v - scale * vr)
            xv = jnp.where(hit, xr * recip, xv - scale * xr)
        out.append(xf * lax.rsqrt(diag))
        if p < 14:
            rest = jnp.concatenate(left[p + 2 :], axis=0)
            group = lax.broadcasted_iota(jnp.int32, rest.shape, 1) // 8
            rest = split(jnp.where(group == p, rest, 0.0))
            wide = [jnp.concatenate([v, xv], axis=1), jnp.zeros((120 - 8 * p, 2 * B), F32)]
            if p > 0:
                wide = [jnp.zeros((8 * p, 2 * B), F32)] + wide
            both = dot_split(rest, split(jnp.concatenate(wide, axis=0)), NN)
        if p < 15:
            q = p + 1
            c = [column_of(left[q], 8 * p + j) for j in range(8)]
            left[q] = left[q] - total([c[j] * row_of(v, j) for j in range(8)])
            right[q] = right[q] - total([c[j] * row_of(xv, j) for j in range(8)])
            for q in range(p + 2, 16):
                rows = slice(8 * (q - p - 2), 8 * (q - p - 1))
                left[q] = left[q] - both[rows, :B]
                right[q] = right[q] - both[rows, B:]
    return jnp.concatenate(out, axis=0)


def total(terms):
    while len(terms) > 1:
        terms = [terms[i] + terms[i + 1] for i in range(0, len(terms), 2)]
    return terms[0]


def at(i):
    return pl.ds(pl.multiple_of(i * B, B), B)


LOWER = [(i, j) for i in range(4) for j in range(i + 1)]


def eliminate(steps, s_ref, l_ref, x_ref):
    def step(k, carry):
        k0 = pl.multiple_of(k * B, B)
        xk = inverse_factor(lambda q: s_ref[pl.ds(pl.multiple_of(k0 + 8 * q, 8), 8), at(k)])
        x_ref[at(k), at(k)] = xk
        xs = split(xk)
        for c in range(*steps):

            @pl.when(k == c)
            def _():
                lo, hi = c * B, (c + 1) * B
                if c > 0:
                    w = dot_split(split(l_ref[lo:hi, :lo]), split(x_ref[:lo, :lo]), NN)
                    x_ref[lo:hi, :lo] = -dot_split(xs, split(w), NN)
                if c < 3:
                    col = dot_split(split(s_ref[hi:, lo:hi]), xs)
                    l_ref[hi:, lo:hi] = col
                    col = split(col)
                    s_ref[hi:, hi:] -= dot_split(col, col)

        return carry

    lax.fori_loop(steps[0], steps[1], step, 0)


def unpack(packed, s_ref):
    for b, (i, j) in enumerate(LOWER):
        s_ref[i * B : (i + 1) * B, j * B : (j + 1) * B] = packed[b * B : (b + 1) * B, :]


def whole_kernel(a_ref, out_ref, s_ref, l_ref, x_ref, sem):
    unpack(a_ref[...].reshape(1280, B), s_ref)
    x_ref[...] = jnp.zeros_like(x_ref)
    eliminate((0, 4), s_ref, l_ref, x_ref)
    copy = pltpu.make_async_copy(x_ref, out_ref, sem)
    copy.start()
    copy.wait()


def first_kernel(ids, mine_ref, theirs_ref, x_ref, s_ref, l_ref, p_ref):
    parity = lax.rem(ids[0], 2)
    p_ref[pl.ds(pl.multiple_of((1 - parity) * 640, 640), 640), :] = mine_ref[:, :40, :].reshape(640, B)
    p_ref[pl.ds(pl.multiple_of(parity * 640, 640), 640), :] = theirs_ref[...].reshape(640, B)
    unpack(p_ref, s_ref)
    x_ref[...] = jnp.zeros_like(x_ref)
    eliminate((0, 3), s_ref, l_ref, x_ref)


def last_kernel(xin_ref, s_ref, l_ref, x_ref):
    x_ref[...] = xin_ref[...]
    eliminate((3, 4), s_ref, l_ref, x_ref)


SQUARE = jax.ShapeDtypeStruct((N, N), F32)
FAR = pl.BlockSpec(memory_space=pltpu.HBM)


def far(x):
    return pltpu.with_memory_space_constraint(x, pltpu.HBM)


def cost(gflop):
    return pl.CostEstimate(flops=int(gflop * 1e9), bytes_accessed=2**21, transcendentals=0)


def inverse_whole(packed):
    return pl.pallas_call(
        whole_kernel,
        out_shape=pltpu.HBM((N, N), F32),
        in_specs=[VMEM],
        out_specs=FAR,
        scratch_shapes=[pltpu.VMEM((N, N), F32)] * 3 + [pltpu.SemaphoreType.DMA],
        compiler_params=PARAMS,
        cost_estimate=cost(25),
    )(packed)


def inverse_first(ids, mine, theirs):
    return pl.pallas_call(
        first_kernel,
        out_shape=[SQUARE] * 3,
        in_specs=[SMEM, VMEM, VMEM],
        out_specs=[VMEM] * 3,
        scratch_shapes=[pltpu.VMEM((1280, B), F32)],
        compiler_params=PARAMS,
        cost_estimate=cost(1),
    )(ids, mine, theirs)


def inverse_last(x, s, l):
    return pl.pallas_call(
        last_kernel,
        out_shape=SQUARE,
        in_specs=[VMEM] * 3,
        out_specs=VMEM,
        compiler_params=PARAMS,
        cost_estimate=cost(6),
    )(x, s, l)


def split(x):
    hi = x.astype(jnp.bfloat16)
    return hi, (x - hi.astype(F32)).astype(jnp.bfloat16)


def dot_split(a, b, dims=NT):
    def dot(u, v):
        return lax.dot_general(u, v, (dims, ((), ())), preferred_element_type=F32)

    return dot(a[0], b[0]) + (dot(a[0], b[1]) + dot(a[1], b[0]))


def symmetric(ref, i, j):
    return 0.5 * (
        ref[i * B : (i + 1) * B, j * B : (j + 1) * B]
        + ref[j * B : (j + 1) * B, i * B : (i + 1) * B].T
    )


def spread_kernel(ids, a_ref, out_ref, p_ref):
    @pl.when(ids[1] > 0)
    def _():
        for c in range(4):
            out_ref[:, 32 * c : 32 * c + 32, :] = a_ref[:, c * B : (c + 1) * B].reshape(16, 32, B)

    @pl.when(ids[1] == 0)
    def _():
        for b, (i, j) in enumerate(LOWER):
            p_ref[b * B : (b + 1) * B, :] = symmetric(a_ref, i, j)
        out_ref[:, :80, :] = p_ref[...].reshape(16, 80, B)
        out_ref[:, 80:, :] = jnp.zeros((16, 48, B), F32)


def spread(ids, columns):
    return pl.pallas_call(
        spread_kernel,
        out_shape=jax.ShapeDtypeStruct((16, B, B), F32),
        in_specs=[SMEM, VMEM],
        out_specs=VMEM,
        scratch_shapes=[pltpu.VMEM((1280, B), F32)],
        compiler_params=PARAMS,
    )(ids, columns)


def place_of(cmap, front, tile, i):
    return cmap[front, jnp.maximum(4 * tile - 4 + i, 0)] - 4 * (tile - 1)


def corner_kernel(
    ids, cmap, a_far, top_ref, x_far, pf_far, panel_ref, keep_ref, send_ref,
    a_ref, x_ref, pf_ref, b_ref, p_ref, sems,
):
    copies = [
        pltpu.make_async_copy(x_far, x_ref, sems.at[0]),
        pltpu.make_async_copy(a_far.at[0, :, pl.ds(0, 2 * N)], a_ref, sems.at[1]),
        pltpu.make_async_copy(pf_far, pf_ref, sems.at[2]),
    ]
    for copy in copies:
        copy.start()
    front, tile = ids[0], ids[1]
    parity = lax.rem(front, 2)
    raw = [top_ref[:, 32 * c : 32 * c + 32, :].reshape(N, B) for c in range(4)]
    raw = split(jnp.concatenate(raw, axis=1))
    copies[0].wait()
    x = split(x_ref[...])
    top = split(dot_split(raw, x))
    copies[1].wait()
    panel_ref[...] = dot_split(split(a_ref[:, :N]), x)
    b_ref[...] = jnp.zeros_like(b_ref)
    for i in range(4):
        rows = slice(i * B, (i + 1) * B)
        first = a_ref[rows, N:] - dot_split(split(panel_ref[rows, :]), top)

        @pl.when(tile > 0)
        def _():
            b_ref[at(place_of(cmap, front, tile, i)), :] = first

    copies[2].wait()

    @pl.when((tile <= 1) & (parity == 1))
    def _():
        b_ref[pl.ds(pl.multiple_of(tile * N, N), N), :] += pf_ref[...]

    for b, (i, j) in enumerate(LOWER):
        p_ref[b * B : (b + 1) * B, :] = symmetric(b_ref, i, j)
    base = jnp.where(tile == 1, N, 0)
    for ref, half in ((keep_ref, 1 - parity), (send_ref, parity)):
        ref[:, :40, :] = p_ref[pl.ds(pl.multiple_of(half * 640, 640), 640), :].reshape(16, 40, B)
        rows = pl.ds(pl.multiple_of(base + half * 256, 256), 256)
        for c in range(4):
            ref[:, 40 + 16 * c : 56 + 16 * c, :] = b_ref[rows, c * B : (c + 1) * B].reshape(16, 16, B)


def corner(ids, cmap, front_vals, tops, x, pf):
    return pl.pallas_call(
        corner_kernel,
        out_shape=[SQUARE] + [jax.ShapeDtypeStruct((16, 104, B), F32)] * 2,
        in_specs=[SMEM, SMEM, FAR, VMEM, FAR, FAR],
        out_specs=[VMEM] * 3,
        scratch_shapes=[
            pltpu.VMEM((N, 2 * N), F32),
            pltpu.VMEM((N, N), F32),
            pltpu.VMEM((N, N), F32),
            pltpu.VMEM((2 * N, N), F32),
            pltpu.VMEM((1280, B), F32),
            pltpu.SemaphoreType.DMA((3,)),
        ],
        compiler_params=PARAMS,
        cost_estimate=cost(3),
    )(ids, cmap, far(front_vals), tops, far(x), far(pf))


def schur_kernel(
    ids, cmap, a_far, panel_far, x_far, top_ref, keep_far, out_far,
    a_ref, panel_ref, x_ref, keep_ref, send_ref, sems,
):
    copies = [
        pltpu.make_async_copy(x_far, x_ref, sems.at[0]),
        pltpu.make_async_copy(panel_far, panel_ref, sems.at[1]),
        pltpu.make_async_copy(a_far.at[0, :, pl.ds(N, 2 * N)], a_ref, sems.at[2]),
    ]
    for copy in copies:
        copy.start()
    front, tile = ids[0], ids[1]
    parity = lax.rem(front, 2)
    keep_ref[...] = jnp.zeros_like(keep_ref)
    send_ref[...] = jnp.zeros_like(send_ref)
    copies[0].wait()
    x = split(x_ref[...])
    tops = []
    for h in range(2):
        raw = [
            top_ref[:, h * B + 32 * c : h * B + 32 * c + 32, :].reshape(N, B) for c in range(4)
        ]
        tops.append(split(dot_split(split(jnp.concatenate(raw, axis=1)), x)))
    copies[1].wait()
    copies[2].wait()
    for i in range(4):
        rows = slice(i * B, (i + 1) * B)
        panel = split(panel_ref[rows, :])
        place = place_of(cmap, front, tile, i)
        first = a_ref[rows, :N] - dot_split(panel, tops[0])
        second = a_ref[rows, N:] - dot_split(panel, tops[1])

        @pl.when((tile > 0) & (parity == 1))
        def _():
            keep_ref[at(place - 1), :] = first
            send_ref[at(place - 1), :] = second

        @pl.when((tile > 0) & (parity == 0))
        def _():
            keep_ref[at(place - 1), :] = second
            send_ref[at(place - 1), :] = first

    copies = [
        pltpu.make_async_copy(send_ref, out_far, sems.at[3]),
        pltpu.make_async_copy(keep_ref, keep_far, sems.at[4]),
    ]
    for copy in copies:
        copy.start()
    for copy in copies:
        copy.wait()


def schur(ids, cmap, front_vals, panel, x, tops):
    return pl.pallas_call(
        schur_kernel,
        out_shape=[pltpu.HBM((6 * B, N), F32)] * 2,
        in_specs=[SMEM, SMEM, FAR, FAR, FAR, VMEM],
        out_specs=[FAR, FAR],
        scratch_shapes=[
            pltpu.VMEM((N, 2 * N), F32),
            pltpu.VMEM((N, N), F32),
            pltpu.VMEM((N, N), F32),
            pltpu.VMEM((6 * B, N), F32),
            pltpu.VMEM((6 * B, N), F32),
            pltpu.SemaphoreType.DMA((5,)),
        ],
        compiler_params=PARAMS,
        cost_estimate=cost(8),
    )(ids, cmap, far(front_vals), far(panel), far(x), tops)


def own_kernel(keep_far, recv_far, lower_ref, upper_ref, buf, sems):
    copies = []
    for h in range(2):
        rows = pl.ds(h * 3 * B, 3 * B)
        for n, ref in enumerate((keep_far, recv_far)):
            copies.append(
                pltpu.make_async_copy(ref.at[rows], buf.at[2 * h + n], sems.at[2 * h + n])
            )
    for copy in copies:
        copy.start()
    for h, ref in enumerate((lower_ref, upper_ref)):
        copies[2 * h].wait()
        copies[2 * h + 1].wait()
        ref[...] = buf[2 * h] + buf[2 * h + 1]


def own_halves(keep, recv):
    return pl.pallas_call(
        own_kernel,
        out_shape=[jax.ShapeDtypeStruct((3 * B, N), F32)] * 2,
        in_specs=[FAR, FAR],
        out_specs=[VMEM, VMEM],
        scratch_shapes=[pltpu.VMEM((4, 3 * B, N), F32), pltpu.SemaphoreType.DMA((4,))],
        compiler_params=PARAMS,
        cost_estimate=cost(1),
    )(far(keep), far(recv))


def parent_kernel(ids, own_ref, other_ref, x_ref, mine_ref, theirs_ref, out_ref):
    x = split(x_ref[...])
    parity = lax.rem(ids[0], 2)

    @pl.when(parity == 1)
    def _():
        out_ref[...] = dot_split(split(own_ref[...]), x)

    @pl.when(parity == 0)
    def _():
        top = [
            jnp.concatenate(
                [
                    theirs_ref[:, 16 * c : 16 * c + 16, :].reshape(256, B),
                    mine_ref[:, 40 + 16 * c : 56 + 16 * c, :].reshape(256, B),
                ],
                axis=0,
            )
            for c in range(4)
        ]
        top = split(dot_split(split(jnp.concatenate(top, axis=1)), x))
        panel = split(dot_split(split(other_ref[...]), x))
        out_ref[...] = own_ref[...] - dot_split(panel, top)


def parent_step(ids, own, other, x, mine, theirs):
    return pl.pallas_call(
        parent_kernel,
        out_shape=SQUARE,
        in_specs=[SMEM] + [VMEM] * 5,
        out_specs=VMEM,
        compiler_params=PARAMS,
        cost_estimate=cost(4),
    )(ids, own, other, x, mine, theirs)


def fan_tops_kernel(parts_ref, out_ref, sems):
    copies = []
    for t in range(16):
        copies.append(
            pltpu.make_async_copy(parts_ref.at[pl.ds(1, 2)], out_ref.at[t], sems.at[t])
        )
    for copy in copies:
        copy.start()
    for copy in copies:
        copy.wait()


def fan_corner_kernel(parts_ref, out_ref, piece_ref, sems):
    piece_ref[:40, :] = parts_ref[0, :40, :] + parts_ref[1, :40, :]
    piece_ref[40:, :] = parts_ref[1, 40:, :] + parts_ref[2, 40:, :]
    copies = []
    for t in range(16):
        copies.append(pltpu.make_async_copy(piece_ref, out_ref.at[t], sems.at[t]))
    for copy in copies:
        copy.start()
    for copy in copies:
        copy.wait()


def fanned(kernel, parts, shape, scratch):
    return pl.pallas_call(
        kernel,
        out_shape=pltpu.HBM(shape, F32),
        in_specs=[VMEM],
        out_specs=pl.BlockSpec(memory_space=pltpu.HBM),
        scratch_shapes=scratch + [pltpu.SemaphoreType.DMA((16,))],
        compiler_params=PARAMS,
    )(parts)


def exchanged(x):
    return lax.all_to_all(x, "tile", 0, 0)


def gathered(piece):
    return exchanged(jnp.broadcast_to(piece[None], (16,) + piece.shape))


def sibling(x):
    return lax.ppermute(x, "front", [(i, i ^ 1) for i in range(16)])


def local(child_front, parent_front, child_map):
    tile = lax.axis_index("tile")
    front = lax.axis_index("front")
    ids = jnp.stack([front, tile]).astype(jnp.int32)
    parent_vals = parent_front[0]

    pieces = exchanged(spread(ids, child_front[0, :, :N]))
    pivot = gathered(pieces[0, :80])
    pieces, pivot = lax.optimization_barrier((pieces, pivot))
    fan = fanned(fan_tops_kernel, pieces, (16, 2, B, B), [])
    fan, pivot = lax.optimization_barrier((fan, pivot))
    tops = exchanged(fan).reshape(16, 2 * B, B)
    child_x = inverse_whole(pivot)
    child_panel, keep, send = corner(ids, child_map, child_front, tops, child_x, parent_vals)
    summed, panel_later = lax.optimization_barrier((keep + sibling(send), child_panel))
    parts = exchanged(summed)
    keep, send = schur(ids, child_map, child_front, panel_later, child_x, tops)
    send, parts = lax.optimization_barrier((send, parts))
    fan = fanned(fan_corner_kernel, parts, (16, 104, B), [pltpu.VMEM((104, B), F32)])
    mine = exchanged(fan)
    lower, upper = own_halves(keep, sibling(send))
    mine, lower = lax.optimization_barrier((mine, lower))
    theirs = sibling(mine[:, :40])
    top_theirs = sibling(mine[:, 40:])
    arrived = lax.ppermute(lower, "tile", [(i, i - 1) for i in range(1, 16)])
    x, s, l = inverse_first(ids, mine, theirs)
    assembled = (
        parent_vals + jnp.pad(upper, ((0, B), (0, 0))) + jnp.pad(arrived, ((B, 0), (0, 0)))
    )
    assembled, _ = lax.optimization_barrier((assembled, x))
    other = sibling(assembled)
    parent_x = inverse_last(x, s, l)
    result = parent_step(ids, assembled, other, parent_x, mine, top_theirs)
    return (child_panel[None], result[None])


def solution(mesh):
    return jax.shard_map(
        local,
        mesh=mesh,
        in_specs=(P("front", "tile", None), P("front", "tile", None), P()),
        out_specs=(P("front", "tile", None), P("front", "tile", None)),
        check_vma=False,
    )
```

```python
import jax
import jax.numpy as jnp
from jax import lax
from jax.experimental import pallas as pl
from jax.experimental.pallas import tpu as pltpu
from jax.sharding import PartitionSpec as P

B = 128
N = 512
NT = ((1,), (1,))
NN = ((1,), (0,))
F32 = jnp.float32
VMEM = pl.BlockSpec(memory_space=pltpu.VMEM)
SMEM = pl.BlockSpec(memory_space=pltpu.SMEM)
PARAMS = pltpu.CompilerParams(vmem_limit_bytes=40 * 1024 * 1024)


def row_of(v, j):
    return jnp.broadcast_to(v[j : j + 1, :], v.shape)


def column_of(v, j):
    return jnp.broadcast_to(v[:, j : j + 1], (v.shape[0], B))


def inverse_factor(rows_at):
    sub = lax.broadcasted_iota(jnp.int32, (8, B), 0)
    lane = lax.broadcasted_iota(jnp.int32, (8, B), 1)
    left = [rows_at(q) for q in range(16)]
    right = [jnp.where(lane == sub + 8 * q, 1.0, 0.0).astype(F32) for q in range(16)]
    out = []
    for p in range(16):
        cols = [column_of(left[p], 8 * p + j) for j in range(8)]
        v, xv = left[p], right[p]
        xf = diag = None
        pivot = row_of(cols[0], 0)
        for j in range(8):
            recip = 1.0 / pivot
            hit = sub == j
            diag = pivot if diag is None else jnp.where(hit, pivot, diag)
            rows = [row_of(cols[m], j) for m in range(j + 1, 8)]
            if j < 7:
                pivot = row_of(cols[j + 1], j + 1) - (rows[0] * rows[0]) * recip
            scale = jnp.where(hit, 0.0, cols[j]) * recip
            for m, cm in zip(range(j + 1, 8), rows):
                cols[m] = jnp.where(hit, cm * recip, cols[m] - scale * cm)
            vr, xr = row_of(v, j), row_of(xv, j)
            xf = xr if xf is None else jnp.where(hit, xr, xf)
            v = jnp.where(hit, vr * recip, v - scale * vr)
            xv = jnp.where(hit, xr * recip, xv - scale * xr)
        out.append(xf * lax.rsqrt(diag))
        if p < 14:
            rest = jnp.concatenate(left[p + 2 :], axis=0)
            group = lax.broadcasted_iota(jnp.int32, rest.shape, 1) // 8
            rest = split(jnp.where(group == p, rest, 0.0))
            wide = [jnp.concatenate([v, xv], axis=1), jnp.zeros((120 - 8 * p, 2 * B), F32)]
            if p > 0:
                wide = [jnp.zeros((8 * p, 2 * B), F32)] + wide
            both = dot_split(rest, split(jnp.concatenate(wide, axis=0)), NN)
        if p < 15:
            q = p + 1
            c = [column_of(left[q], 8 * p + j) for j in range(8)]
            left[q] = left[q] - total([c[j] * row_of(v, j) for j in range(8)])
            right[q] = right[q] - total([c[j] * row_of(xv, j) for j in range(8)])
            for q in range(p + 2, 16):
                rows = slice(8 * (q - p - 2), 8 * (q - p - 1))
                left[q] = left[q] - both[rows, :B]
                right[q] = right[q] - both[rows, B:]
    return jnp.concatenate(out, axis=0)


def total(terms):
    while len(terms) > 1:
        terms = [terms[i] + terms[i + 1] for i in range(0, len(terms), 2)]
    return terms[0]


def at(i):
    return pl.ds(pl.multiple_of(i * B, B), B)


LOWER = [(i, j) for i in range(4) for j in range(i + 1)]


def eliminate(steps, s_ref, l_ref, x_ref):
    def step(k, carry):
        k0 = pl.multiple_of(k * B, B)
        xk = inverse_factor(lambda q: s_ref[pl.ds(pl.multiple_of(k0 + 8 * q, 8), 8), at(k)])
        x_ref[at(k), at(k)] = xk
        xs = split(xk)
        for c in range(*steps):

            @pl.when(k == c)
            def _():
                lo, hi = c * B, (c + 1) * B
                if c > 0:
                    w = dot_split(split(l_ref[lo:hi, :lo]), split(x_ref[:lo, :lo]), NN)
                    x_ref[lo:hi, :lo] = -dot_split(xs, split(w), NN)
                if c < 3:
                    col = dot_split(split(s_ref[hi:, lo:hi]), xs)
                    l_ref[hi:, lo:hi] = col
                    col = split(col)
                    s_ref[hi:, hi:] -= dot_split(col, col)

        return carry

    lax.fori_loop(steps[0], steps[1], step, 0)


def unpack(packed, s_ref):
    for b, (i, j) in enumerate(LOWER):
        s_ref[i * B : (i + 1) * B, j * B : (j + 1) * B] = packed[b * B : (b + 1) * B, :]


def whole_kernel(a_ref, out_ref, s_ref, l_ref, x_ref, sem):
    unpack(a_ref[...].reshape(1280, B), s_ref)
    x_ref[...] = jnp.zeros_like(x_ref)
    eliminate((0, 4), s_ref, l_ref, x_ref)
    copy = pltpu.make_async_copy(x_ref, out_ref, sem)
    copy.start()
    copy.wait()


def first_kernel(ids, mine_ref, theirs_ref, x_ref, s_ref, l_ref, p_ref):
    parity = lax.rem(ids[0], 2)
    p_ref[pl.ds(pl.multiple_of((1 - parity) * 640, 640), 640), :] = mine_ref[:, :40, :].reshape(640, B)
    p_ref[pl.ds(pl.multiple_of(parity * 640, 640), 640), :] = theirs_ref[...].reshape(640, B)
    unpack(p_ref, s_ref)
    x_ref[...] = jnp.zeros_like(x_ref)
    eliminate((0, 3), s_ref, l_ref, x_ref)


def last_kernel(xin_ref, s_ref, l_ref, x_ref):
    x_ref[...] = xin_ref[...]
    eliminate((3, 4), s_ref, l_ref, x_ref)


SQUARE = jax.ShapeDtypeStruct((N, N), F32)
FAR = pl.BlockSpec(memory_space=pltpu.HBM)


def far(x):
    return pltpu.with_memory_space_constraint(x, pltpu.HBM)


def cost(gflop):
    return pl.CostEstimate(flops=int(gflop * 1e9), bytes_accessed=2**21, transcendentals=0)


def inverse_whole(packed):
    return pl.pallas_call(
        whole_kernel,
        out_shape=pltpu.HBM((N, N), F32),
        in_specs=[VMEM],
        out_specs=FAR,
        scratch_shapes=[pltpu.VMEM((N, N), F32)] * 3 + [pltpu.SemaphoreType.DMA],
        compiler_params=PARAMS,
        cost_estimate=cost(25),
    )(packed)


def inverse_first(ids, mine, theirs):
    return pl.pallas_call(
        first_kernel,
        out_shape=[SQUARE] * 3,
        in_specs=[SMEM, VMEM, VMEM],
        out_specs=[VMEM] * 3,
        scratch_shapes=[pltpu.VMEM((1280, B), F32)],
        compiler_params=PARAMS,
        cost_estimate=cost(1),
    )(ids, mine, theirs)


def inverse_last(x, s, l):
    return pl.pallas_call(
        last_kernel,
        out_shape=SQUARE,
        in_specs=[VMEM] * 3,
        out_specs=VMEM,
        compiler_params=PARAMS,
        cost_estimate=cost(6),
    )(x, s, l)


def split(x):
    hi = x.astype(jnp.bfloat16)
    return hi, (x - hi.astype(F32)).astype(jnp.bfloat16)


def dot_split(a, b, dims=NT):
    def dot(u, v):
        return lax.dot_general(u, v, (dims, ((), ())), preferred_element_type=F32)

    return dot(a[0], b[0]) + (dot(a[0], b[1]) + dot(a[1], b[0]))


def symmetric(ref, i, j):
    return 0.5 * (
        ref[i * B : (i + 1) * B, j * B : (j + 1) * B]
        + ref[j * B : (j + 1) * B, i * B : (i + 1) * B].T
    )


def spread_kernel(ids, a_far, out_ref, a_ref, p_ref, sem):
    copy = pltpu.make_async_copy(a_far.at[0, :, pl.ds(0, N)], a_ref, sem)
    copy.start()
    copy.wait()

    @pl.when(ids[1] > 0)
    def _():
        for c in range(4):
            out_ref[:, 32 * c : 32 * c + 32, :] = a_ref[:, c * B : (c + 1) * B].reshape(16, 32, B)

    @pl.when(ids[1] == 0)
    def _():
        for b, (i, j) in enumerate(LOWER):
            p_ref[b * B : (b + 1) * B, :] = symmetric(a_ref, i, j)
        out_ref[:, :80, :] = p_ref[...].reshape(16, 80, B)
        out_ref[:, 80:, :] = jnp.zeros((16, 48, B), F32)


def spread(ids, front_vals):
    return pl.pallas_call(
        spread_kernel,
        out_shape=jax.ShapeDtypeStruct((16, B, B), F32),
        in_specs=[SMEM, FAR],
        out_specs=VMEM,
        scratch_shapes=[
            pltpu.VMEM((N, N), F32),
            pltpu.VMEM((1280, B), F32),
            pltpu.SemaphoreType.DMA,
        ],
        compiler_params=PARAMS,
    )(ids, far(front_vals))


def place_of(cmap, front, tile, i):
    return cmap[front, jnp.maximum(4 * tile - 4 + i, 0)] - 4 * (tile - 1)


def panel_kernel(a_far, x_far, out_far, a_ref, x_ref, panel_ref, sems):
    copies = [
        pltpu.make_async_copy(x_far, x_ref, sems.at[0]),
        pltpu.make_async_copy(a_far.at[0, :, pl.ds(0, N)], a_ref, sems.at[1]),
    ]
    for copy in copies:
        copy.start()
    for copy in copies:
        copy.wait()
    panel_ref[...] = dot_split(split(a_ref[...]), split(x_ref[...]))
    copy = pltpu.make_async_copy(panel_ref, out_far, sems.at[2])
    copy.start()
    copy.wait()


def panel_of(front_vals, x):
    return pl.pallas_call(
        panel_kernel,
        out_shape=pltpu.HBM((N, N), F32),
        in_specs=[FAR, FAR],
        out_specs=FAR,
        scratch_shapes=[pltpu.VMEM((N, N), F32)] * 3 + [pltpu.SemaphoreType.DMA((3,))],
        compiler_params=PARAMS,
        cost_estimate=cost(1),
    )(far(front_vals), far(x))


def corner_kernel(
    ids, cmap, a_far, panel_far, top_ref, x_far, pf_far, keep_ref, send_ref,
    a_ref, panel_ref, x_ref, pf_ref, b_ref, p_ref, sems,
):
    copies = [
        pltpu.make_async_copy(x_far, x_ref, sems.at[0]),
        pltpu.make_async_copy(panel_far, panel_ref, sems.at[1]),
        pltpu.make_async_copy(a_far.at[0, :, pl.ds(N, N)], a_ref, sems.at[2]),
        pltpu.make_async_copy(pf_far, pf_ref, sems.at[3]),
    ]
    for copy in copies:
        copy.start()
    front, tile = ids[0], ids[1]
    parity = lax.rem(front, 2)
    raw = [top_ref[:, 32 * c : 32 * c + 32, :].reshape(N, B) for c in range(4)]
    raw = split(jnp.concatenate(raw, axis=1))
    copies[0].wait()
    top = split(dot_split(raw, split(x_ref[...])))
    copies[1].wait()
    copies[2].wait()
    b_ref[...] = jnp.zeros_like(b_ref)
    for i in range(4):
        rows = slice(i * B, (i + 1) * B)
        first = a_ref[rows, :] - dot_split(split(panel_ref[rows, :]), top)

        @pl.when(tile > 0)
        def _():
            b_ref[at(place_of(cmap, front, tile, i)), :] = first

    copies[3].wait()

    @pl.when((tile <= 1) & (parity == 1))
    def _():
        b_ref[pl.ds(pl.multiple_of(tile * N, N), N), :] += pf_ref[...]

    for b, (i, j) in enumerate(LOWER):
        p_ref[b * B : (b + 1) * B, :] = symmetric(b_ref, i, j)
    base = jnp.where(tile == 1, N, 0)
    for ref, half in ((keep_ref, 1 - parity), (send_ref, parity)):
        ref[:, :40, :] = p_ref[pl.ds(pl.multiple_of(half * 640, 640), 640), :].reshape(16, 40, B)
        rows = pl.ds(pl.multiple_of(base + half * 256, 256), 256)
        for c in range(4):
            ref[:, 40 + 16 * c : 56 + 16 * c, :] = b_ref[rows, c * B : (c + 1) * B].reshape(16, 16, B)


def corner(ids, cmap, front_vals, panel, tops, x, pf):
    return pl.pallas_call(
        corner_kernel,
        out_shape=[jax.ShapeDtypeStruct((16, 104, B), F32)] * 2,
        in_specs=[SMEM, SMEM, FAR, FAR, VMEM, FAR, FAR],
        out_specs=[VMEM] * 2,
        scratch_shapes=[pltpu.VMEM((N, N), F32)] * 4
        + [
            pltpu.VMEM((2 * N, N), F32),
            pltpu.VMEM((1280, B), F32),
            pltpu.SemaphoreType.DMA((4,)),
        ],
        compiler_params=PARAMS,
        cost_estimate=cost(3),
    )(ids, cmap, far(front_vals), far(panel), tops, far(x), far(pf))


def schur_kernel(
    ids, cmap, a_far, panel_far, x_far, top_ref, keep_far, out_far,
    a_ref, panel_ref, x_ref, keep_ref, send_ref, sems,
):
    copies = [
        pltpu.make_async_copy(x_far, x_ref, sems.at[0]),
        pltpu.make_async_copy(panel_far, panel_ref, sems.at[1]),
        pltpu.make_async_copy(a_far.at[0, :, pl.ds(N, 2 * N)], a_ref, sems.at[2]),
    ]
    for copy in copies:
        copy.start()
    front, tile = ids[0], ids[1]
    parity = lax.rem(front, 2)
    keep_ref[...] = jnp.zeros_like(keep_ref)
    send_ref[...] = jnp.zeros_like(send_ref)
    copies[0].wait()
    x = split(x_ref[...])
    tops = []
    for h in range(2):
        raw = [
            top_ref[:, h * B + 32 * c : h * B + 32 * c + 32, :].reshape(N, B) for c in range(4)
        ]
        tops.append(split(dot_split(split(jnp.concatenate(raw, axis=1)), x)))
    copies[1].wait()
    copies[2].wait()
    for i in range(4):
        rows = slice(i * B, (i + 1) * B)
        panel = split(panel_ref[rows, :])
        place = place_of(cmap, front, tile, i)
        first = a_ref[rows, :N] - dot_split(panel, tops[0])
        second = a_ref[rows, N:] - dot_split(panel, tops[1])

        @pl.when((tile > 0) & (parity == 1))
        def _():
            keep_ref[at(place - 1), :] = first
            send_ref[at(place - 1), :] = second

        @pl.when((tile > 0) & (parity == 0))
        def _():
            keep_ref[at(place - 1), :] = second
            send_ref[at(place - 1), :] = first

    copies = [
        pltpu.make_async_copy(send_ref, out_far, sems.at[3]),
        pltpu.make_async_copy(keep_ref, keep_far, sems.at[4]),
    ]
    for copy in copies:
        copy.start()
    for copy in copies:
        copy.wait()


def schur(ids, cmap, front_vals, panel, x, tops):
    return pl.pallas_call(
        schur_kernel,
        out_shape=[pltpu.HBM((6 * B, N), F32)] * 2,
        in_specs=[SMEM, SMEM, FAR, FAR, FAR, VMEM],
        out_specs=[FAR, FAR],
        scratch_shapes=[
            pltpu.VMEM((N, 2 * N), F32),
            pltpu.VMEM((N, N), F32),
            pltpu.VMEM((N, N), F32),
            pltpu.VMEM((6 * B, N), F32),
            pltpu.VMEM((6 * B, N), F32),
            pltpu.SemaphoreType.DMA((5,)),
        ],
        compiler_params=PARAMS,
        cost_estimate=cost(8),
    )(ids, cmap, far(front_vals), far(panel), far(x), tops)


def own_kernel(keep_far, recv_far, lower_ref, upper_ref, buf, sems):
    copies = []
    for h in range(2):
        rows = pl.ds(h * 3 * B, 3 * B)
        for n, ref in enumerate((keep_far, recv_far)):
            copies.append(
                pltpu.make_async_copy(ref.at[rows], buf.at[2 * h + n], sems.at[2 * h + n])
            )
    for copy in copies:
        copy.start()
    for h, ref in enumerate((lower_ref, upper_ref)):
        copies[2 * h].wait()
        copies[2 * h + 1].wait()
        ref[...] = buf[2 * h] + buf[2 * h + 1]


def own_halves(keep, recv):
    return pl.pallas_call(
        own_kernel,
        out_shape=[jax.ShapeDtypeStruct((3 * B, N), F32)] * 2,
        in_specs=[FAR, FAR],
        out_specs=[VMEM, VMEM],
        scratch_shapes=[pltpu.VMEM((4, 3 * B, N), F32), pltpu.SemaphoreType.DMA((4,))],
        compiler_params=PARAMS,
        cost_estimate=cost(1),
    )(far(keep), far(recv))


def parent_kernel(ids, own_ref, other_ref, x_ref, mine_ref, theirs_ref, out_ref):
    x = split(x_ref[...])
    parity = lax.rem(ids[0], 2)

    @pl.when(parity == 1)
    def _():
        out_ref[...] = dot_split(split(own_ref[...]), x)

    @pl.when(parity == 0)
    def _():
        top = [
            jnp.concatenate(
                [
                    theirs_ref[:, 16 * c : 16 * c + 16, :].reshape(256, B),
                    mine_ref[:, 40 + 16 * c : 56 + 16 * c, :].reshape(256, B),
                ],
                axis=0,
            )
            for c in range(4)
        ]
        top = split(dot_split(split(jnp.concatenate(top, axis=1)), x))
        panel = split(dot_split(split(other_ref[...]), x))
        out_ref[...] = own_ref[...] - dot_split(panel, top)


def parent_step(ids, own, other, x, mine, theirs):
    return pl.pallas_call(
        parent_kernel,
        out_shape=SQUARE,
        in_specs=[SMEM] + [VMEM] * 5,
        out_specs=VMEM,
        compiler_params=PARAMS,
        cost_estimate=cost(4),
    )(ids, own, other, x, mine, theirs)


def fan_tops_kernel(parts_ref, out_ref, sems):
    copies = []
    for t in range(16):
        copies.append(
            pltpu.make_async_copy(parts_ref.at[pl.ds(1, 2)], out_ref.at[t], sems.at[t])
        )
    for copy in copies:
        copy.start()
    for copy in copies:
        copy.wait()


def fan_corner_kernel(parts_ref, out_ref, piece_ref, sems):
    piece_ref[:40, :] = parts_ref[0, :40, :] + parts_ref[1, :40, :]
    piece_ref[40:, :] = parts_ref[1, 40:, :] + parts_ref[2, 40:, :]
    copies = []
    for t in range(16):
        copies.append(pltpu.make_async_copy(piece_ref, out_ref.at[t], sems.at[t]))
    for copy in copies:
        copy.start()
    for copy in copies:
        copy.wait()


def fanned(kernel, parts, shape, scratch):
    return pl.pallas_call(
        kernel,
        out_shape=pltpu.HBM(shape, F32),
        in_specs=[VMEM],
        out_specs=pl.BlockSpec(memory_space=pltpu.HBM),
        scratch_shapes=scratch + [pltpu.SemaphoreType.DMA((16,))],
        compiler_params=PARAMS,
    )(parts)


def exchanged(x):
    return lax.all_to_all(x, "tile", 0, 0)


def gathered(piece):
    return exchanged(jnp.broadcast_to(piece[None], (16,) + piece.shape))


def sibling(x):
    return lax.ppermute(x, "front", [(i, i ^ 1) for i in range(16)])


def local(child_front, parent_front, child_map):
    tile = lax.axis_index("tile")
    front = lax.axis_index("front")
    ids = jnp.stack([front, tile]).astype(jnp.int32)
    parent_vals = parent_front[0]

    pieces = exchanged(spread(ids, child_front))
    pivot = gathered(pieces[0, :80])
    pieces, pivot = lax.optimization_barrier((pieces, pivot))
    fan = fanned(fan_tops_kernel, pieces, (16, 2, B, B), [])
    fan, pivot = lax.optimization_barrier((fan, pivot))
    tops = exchanged(fan).reshape(16, 2 * B, B)
    child_x = inverse_whole(pivot)
    child_panel = panel_of(child_front, child_x)
    keep, send = corner(ids, child_map, child_front, child_panel, tops, child_x, parent_vals)
    summed, panel_later = lax.optimization_barrier((keep + sibling(send), child_panel))
    parts = exchanged(summed)
    keep, send = schur(ids, child_map, child_front, panel_later, child_x, tops)
    send, parts = lax.optimization_barrier((send, parts))
    fan = fanned(fan_corner_kernel, parts, (16, 104, B), [pltpu.VMEM((104, B), F32)])
    mine = exchanged(fan)
    lower, upper = own_halves(keep, sibling(send))
    mine, _ = lax.optimization_barrier((mine, lower))
    theirs = sibling(mine[:, :40])
    top_theirs = sibling(mine[:, 40:])
    arrived = lax.ppermute(lower, "tile", [(i, i - 1) for i in range(1, 16)])
    x, s, l = inverse_first(ids, mine, theirs)
    assembled = (
        parent_vals + jnp.pad(upper, ((0, B), (0, 0))) + jnp.pad(arrived, ((B, 0), (0, 0)))
    )
    assembled, _ = lax.optimization_barrier((assembled, x))
    other = sibling(assembled)
    parent_x = inverse_last(x, s, l)
    result = parent_step(ids, assembled, other, parent_x, mine, top_theirs)
    return (child_panel[None], result[None])


def solution(mesh):
    return jax.shard_map(
        local,
        mesh=mesh,
        in_specs=(P("front", "tile", None), P("front", "tile", None), P()),
        out_specs=(P("front", "tile", None), P("front", "tile", None)),
        check_vma=False,
    )
```

```python
import jax
import jax.numpy as jnp
from jax import lax
from jax.experimental import pallas as pl
from jax.experimental.pallas import tpu as pltpu
from jax.sharding import PartitionSpec as P

B = 128
N = 512
NT = ((1,), (1,))
NN = ((1,), (0,))
F32 = jnp.float32
VMEM = pl.BlockSpec(memory_space=pltpu.VMEM)
SMEM = pl.BlockSpec(memory_space=pltpu.SMEM)
PARAMS = pltpu.CompilerParams(vmem_limit_bytes=40 * 1024 * 1024)


def row_of(v, j):
    return jnp.broadcast_to(v[j : j + 1, :], v.shape)


def column_of(v, j):
    return jnp.broadcast_to(v[:, j : j + 1], (v.shape[0], B))


def inverse_factor(rows_at):
    sub = lax.broadcasted_iota(jnp.int32, (8, B), 0)
    lane = lax.broadcasted_iota(jnp.int32, (8, B), 1)
    left = [rows_at(q) for q in range(16)]
    right = [jnp.where(lane == sub + 8 * q, 1.0, 0.0).astype(F32) for q in range(16)]
    out = []
    for p in range(16):
        cols = [column_of(left[p], 8 * p + j) for j in range(8)]
        v, xv = left[p], right[p]
        xf = diag = None
        pivot = row_of(cols[0], 0)
        for j in range(8):
            recip = 1.0 / pivot
            hit = sub == j
            diag = pivot if diag is None else jnp.where(hit, pivot, diag)
            rows = [row_of(cols[m], j) for m in range(j + 1, 8)]
            if j < 7:
                pivot = row_of(cols[j + 1], j + 1) - (rows[0] * rows[0]) * recip
            scale = jnp.where(hit, 0.0, cols[j]) * recip
            for m, cm in zip(range(j + 1, 8), rows):
                cols[m] = jnp.where(hit, cm * recip, cols[m] - scale * cm)
            vr, xr = row_of(v, j), row_of(xv, j)
            xf = xr if xf is None else jnp.where(hit, xr, xf)
            v = jnp.where(hit, vr * recip, v - scale * vr)
            xv = jnp.where(hit, xr * recip, xv - scale * xr)
        out.append(xf * lax.rsqrt(diag))
        if p < 14:
            rest = jnp.concatenate(left[p + 2 :], axis=0)
            group = lax.broadcasted_iota(jnp.int32, rest.shape, 1) // 8
            rest = split(jnp.where(group == p, rest, 0.0))
            wide = [jnp.concatenate([v, xv], axis=1), jnp.zeros((120 - 8 * p, 2 * B), F32)]
            if p > 0:
                wide = [jnp.zeros((8 * p, 2 * B), F32)] + wide
            both = dot_split(rest, split(jnp.concatenate(wide, axis=0)), NN)
        if p < 15:
            q = p + 1
            c = [column_of(left[q], 8 * p + j) for j in range(8)]
            left[q] = left[q] - total([c[j] * row_of(v, j) for j in range(8)])
            right[q] = right[q] - total([c[j] * row_of(xv, j) for j in range(8)])
            for q in range(p + 2, 16):
                rows = slice(8 * (q - p - 2), 8 * (q - p - 1))
                left[q] = left[q] - both[rows, :B]
                right[q] = right[q] - both[rows, B:]
    return jnp.concatenate(out, axis=0)


def total(terms):
    while len(terms) > 1:
        terms = [terms[i] + terms[i + 1] for i in range(0, len(terms), 2)]
    return terms[0]


def at(i):
    return pl.ds(pl.multiple_of(i * B, B), B)


LOWER = [(i, j) for i in range(4) for j in range(i + 1)]


def eliminate(steps, s_ref, l_ref, x_ref):
    def step(k, carry):
        k0 = pl.multiple_of(k * B, B)
        xk = inverse_factor(lambda q: s_ref[pl.ds(pl.multiple_of(k0 + 8 * q, 8), 8), at(k)])
        x_ref[at(k), at(k)] = xk
        xs = split(xk)
        for c in range(*steps):

            @pl.when(k == c)
            def _():
                lo, hi = c * B, (c + 1) * B
                if c > 0:
                    w = dot_split(split(l_ref[lo:hi, :lo]), split(x_ref[:lo, :lo]), NN)
                    x_ref[lo:hi, :lo] = -dot_split(xs, split(w), NN)
                if c < 3:
                    col = dot_split(split(s_ref[hi:, lo:hi]), xs)
                    l_ref[hi:, lo:hi] = col
                    col = split(col)
                    s_ref[hi:, hi:] -= dot_split(col, col)

        return carry

    lax.fori_loop(steps[0], steps[1], step, 0)


def unpack(packed, s_ref):
    for b, (i, j) in enumerate(LOWER):
        s_ref[i * B : (i + 1) * B, j * B : (j + 1) * B] = packed[b * B : (b + 1) * B, :]


def whole_kernel(a_ref, out_ref, s_ref, l_ref, x_ref, sem):
    unpack(a_ref[...].reshape(1280, B), s_ref)
    x_ref[...] = jnp.zeros_like(x_ref)
    eliminate((0, 4), s_ref, l_ref, x_ref)
    wait_for(*start_copies([(x_ref, out_ref)], sem))


def first_kernel(ids, mine_ref, theirs_ref, x_ref, s_ref, l_ref, p_ref):
    parity = lax.rem(ids[0], 2)
    p_ref[pl.ds(pl.multiple_of((1 - parity) * 640, 640), 640), :] = mine_ref[:, :40, :].reshape(640, B)
    p_ref[pl.ds(pl.multiple_of(parity * 640, 640), 640), :] = theirs_ref[...].reshape(640, B)
    unpack(p_ref, s_ref)
    x_ref[...] = jnp.zeros_like(x_ref)
    eliminate((0, 3), s_ref, l_ref, x_ref)


def last_kernel(xin_ref, s_ref, l_ref, x_ref):
    x_ref[...] = xin_ref[...]
    eliminate((3, 4), s_ref, l_ref, x_ref)


SQUARE = jax.ShapeDtypeStruct((N, N), F32)
FAR = pl.BlockSpec(memory_space=pltpu.HBM)


PARTS = 4


def start_copies(pairs, sems, first=0):
    groups = []
    for n, (src, dst) in enumerate(pairs):
        step = dst.shape[0] // PARTS
        group = []
        for p in range(PARTS):
            rows = pl.ds(p * step, step)
            sem = sems.at[first + n * PARTS + p]
            group.append(pltpu.make_async_copy(src.at[rows], dst.at[rows], sem))
        groups.append(group)
    for group in groups:
        for copy in group:
            copy.start()
    return groups


def wait_for(*groups):
    for group in groups:
        for copy in group:
            copy.wait()


def far(x):
    return pltpu.with_memory_space_constraint(x, pltpu.HBM)


def cost(gflop):
    return pl.CostEstimate(flops=int(gflop * 1e9), bytes_accessed=2**21, transcendentals=0)


def inverse_whole(packed):
    return pl.pallas_call(
        whole_kernel,
        out_shape=pltpu.HBM((N, N), F32),
        in_specs=[VMEM],
        out_specs=FAR,
        scratch_shapes=[pltpu.VMEM((N, N), F32)] * 3 + [pltpu.SemaphoreType.DMA((PARTS,))],
        compiler_params=PARAMS,
        cost_estimate=cost(25),
    )(packed)


def inverse_first(ids, mine, theirs):
    return pl.pallas_call(
        first_kernel,
        out_shape=[SQUARE] * 3,
        in_specs=[SMEM, VMEM, VMEM],
        out_specs=[VMEM] * 3,
        scratch_shapes=[pltpu.VMEM((1280, B), F32)],
        compiler_params=PARAMS,
        cost_estimate=cost(1),
    )(ids, mine, theirs)


def inverse_last(x, s, l):
    return pl.pallas_call(
        last_kernel,
        out_shape=SQUARE,
        in_specs=[VMEM] * 3,
        out_specs=VMEM,
        compiler_params=PARAMS,
        cost_estimate=cost(6),
    )(x, s, l)


def split(x):
    hi = x.astype(jnp.bfloat16)
    return hi, (x - hi.astype(F32)).astype(jnp.bfloat16)


def dot_split(a, b, dims=NT):
    def dot(u, v):
        return lax.dot_general(u, v, (dims, ((), ())), preferred_element_type=F32)

    return dot(a[0], b[0]) + (dot(a[0], b[1]) + dot(a[1], b[0]))


def symmetric(ref, i, j):
    return 0.5 * (
        ref[i * B : (i + 1) * B, j * B : (j + 1) * B]
        + ref[j * B : (j + 1) * B, i * B : (i + 1) * B].T
    )


def spread_kernel(ids, a_far, out_ref, a_ref, p_ref, sem):
    wait_for(*start_copies([(a_far.at[0, :, pl.ds(0, N)], a_ref)], sem))

    @pl.when(ids[1] > 0)
    def _():
        for c in range(4):
            out_ref[:, 32 * c : 32 * c + 32, :] = a_ref[:, c * B : (c + 1) * B].reshape(16, 32, B)

    @pl.when(ids[1] == 0)
    def _():
        for b, (i, j) in enumerate(LOWER):
            p_ref[b * B : (b + 1) * B, :] = symmetric(a_ref, i, j)
        out_ref[:, :80, :] = p_ref[...].reshape(16, 80, B)
        out_ref[:, 80:, :] = jnp.zeros((16, 48, B), F32)


def spread(ids, front_vals):
    return pl.pallas_call(
        spread_kernel,
        out_shape=jax.ShapeDtypeStruct((16, B, B), F32),
        in_specs=[SMEM, FAR],
        out_specs=VMEM,
        scratch_shapes=[
            pltpu.VMEM((N, N), F32),
            pltpu.VMEM((1280, B), F32),
            pltpu.SemaphoreType.DMA((PARTS,)),
        ],
        compiler_params=PARAMS,
    )(ids, far(front_vals))


def place_of(cmap, front, tile, i):
    return cmap[front, jnp.maximum(4 * tile - 4 + i, 0)] - 4 * (tile - 1)


def panel_kernel(a_far, x_far, out_far, a_ref, x_ref, panel_ref, sems):
    pairs = [(x_far, x_ref), (a_far.at[0, :, pl.ds(0, N)], a_ref)]
    wait_for(*start_copies(pairs, sems))
    panel_ref[...] = dot_split(split(a_ref[...]), split(x_ref[...]))
    wait_for(*start_copies([(panel_ref, out_far)], sems, 2 * PARTS))


def panel_of(front_vals, x):
    return pl.pallas_call(
        panel_kernel,
        out_shape=pltpu.HBM((N, N), F32),
        in_specs=[FAR, FAR],
        out_specs=FAR,
        scratch_shapes=[pltpu.VMEM((N, N), F32)] * 3 + [pltpu.SemaphoreType.DMA((3 * PARTS,))],
        compiler_params=PARAMS,
        cost_estimate=cost(1),
    )(far(front_vals), far(x))


def corner_kernel(
    ids, cmap, a_far, panel_far, top_ref, x_far, pf_far, keep_ref, send_ref,
    a_ref, panel_ref, x_ref, pf_ref, b_ref, p_ref, sems,
):
    copies = start_copies(
        [
            (x_far, x_ref),
            (panel_far, panel_ref),
            (a_far.at[0, :, pl.ds(N, N)], a_ref),
            (pf_far, pf_ref),
        ],
        sems,
    )
    front, tile = ids[0], ids[1]
    parity = lax.rem(front, 2)
    raw = [top_ref[:, 32 * c : 32 * c + 32, :].reshape(N, B) for c in range(4)]
    raw = split(jnp.concatenate(raw, axis=1))
    wait_for(copies[0])
    top = split(dot_split(raw, split(x_ref[...])))
    wait_for(*copies[1:3])
    b_ref[...] = jnp.zeros_like(b_ref)
    for i in range(4):
        rows = slice(i * B, (i + 1) * B)
        first = a_ref[rows, :] - dot_split(split(panel_ref[rows, :]), top)

        @pl.when(tile > 0)
        def _():
            b_ref[at(place_of(cmap, front, tile, i)), :] = first

    wait_for(copies[3])

    @pl.when((tile <= 1) & (parity == 1))
    def _():
        b_ref[pl.ds(pl.multiple_of(tile * N, N), N), :] += pf_ref[...]

    for b, (i, j) in enumerate(LOWER):
        p_ref[b * B : (b + 1) * B, :] = symmetric(b_ref, i, j)
    base = jnp.where(tile == 1, N, 0)
    for ref, half in ((keep_ref, 1 - parity), (send_ref, parity)):
        ref[:, :40, :] = p_ref[pl.ds(pl.multiple_of(half * 640, 640), 640), :].reshape(16, 40, B)
        rows = pl.ds(pl.multiple_of(base + half * 256, 256), 256)
        for c in range(4):
            ref[:, 40 + 16 * c : 56 + 16 * c, :] = b_ref[rows, c * B : (c + 1) * B].reshape(16, 16, B)


def corner(ids, cmap, front_vals, panel, tops, x, pf):
    return pl.pallas_call(
        corner_kernel,
        out_shape=[jax.ShapeDtypeStruct((16, 104, B), F32)] * 2,
        in_specs=[SMEM, SMEM, FAR, FAR, VMEM, FAR, FAR],
        out_specs=[VMEM] * 2,
        scratch_shapes=[pltpu.VMEM((N, N), F32)] * 4
        + [
            pltpu.VMEM((2 * N, N), F32),
            pltpu.VMEM((1280, B), F32),
            pltpu.SemaphoreType.DMA((4 * PARTS,)),
        ],
        compiler_params=PARAMS,
        cost_estimate=cost(3),
    )(ids, cmap, far(front_vals), far(panel), tops, far(x), far(pf))


def schur_kernel(
    ids, cmap, a_far, panel_far, x_far, top_ref, keep_far, out_far,
    a_ref, panel_ref, x_ref, keep_ref, send_ref, sems,
):
    copies = start_copies(
        [(x_far, x_ref), (panel_far, panel_ref), (a_far.at[0, :, pl.ds(N, 2 * N)], a_ref)], sems
    )
    front, tile = ids[0], ids[1]
    parity = lax.rem(front, 2)
    keep_ref[...] = jnp.zeros_like(keep_ref)
    send_ref[...] = jnp.zeros_like(send_ref)
    wait_for(copies[0])
    x = split(x_ref[...])
    out = []
    for h, half, ref, target in (
        (0, parity, send_ref, out_far),
        (1, 1 - parity, keep_ref, keep_far),
    ):
        raw = [
            top_ref[:, pl.ds(pl.multiple_of(half * B + 32 * c, 32), 32), :].reshape(N, B)
            for c in range(4)
        ]
        top = split(dot_split(split(jnp.concatenate(raw, axis=1)), x))
        if h == 0:
            wait_for(*copies[1:])
        for i in range(4):
            rows = slice(i * B, (i + 1) * B)
            rest = a_ref[rows, pl.ds(pl.multiple_of(half * N, N), N)]
            rest = rest - dot_split(split(panel_ref[rows, :]), top)

            @pl.when(tile > 0)
            def _():
                ref[at(place_of(cmap, front, tile, i) - 1), :] = rest

        out += start_copies([(ref, target)], sems, (3 + h) * PARTS)
    wait_for(*out)


def schur(ids, cmap, front_vals, panel, x, tops):
    return pl.pallas_call(
        schur_kernel,
        out_shape=[pltpu.HBM((6 * B, N), F32)] * 2,
        in_specs=[SMEM, SMEM, FAR, FAR, FAR, VMEM],
        out_specs=[FAR, FAR],
        scratch_shapes=[
            pltpu.VMEM((N, 2 * N), F32),
            pltpu.VMEM((N, N), F32),
            pltpu.VMEM((N, N), F32),
            pltpu.VMEM((6 * B, N), F32),
            pltpu.VMEM((6 * B, N), F32),
            pltpu.SemaphoreType.DMA((5 * PARTS,)),
        ],
        compiler_params=PARAMS,
        cost_estimate=cost(8),
    )(ids, cmap, far(front_vals), far(panel), far(x), tops)


def own_kernel(keep_far, recv_far, pf_far, lower_ref, base_ref, buf, pf_ref, sems):
    copies = []
    for h in range(2):
        rows = pl.ds(h * 3 * B, 3 * B)
        for n, ref in enumerate((keep_far, recv_far)):
            copies.append(
                pltpu.make_async_copy(ref.at[rows], buf.at[2 * h + n], sems.at[2 * h + n])
            )
    copies.append(pltpu.make_async_copy(pf_far, pf_ref, sems.at[4]))
    for copy in copies:
        copy.start()
    copies[0].wait()
    copies[1].wait()
    lower_ref[...] = buf[0] + buf[1]
    copies[2].wait()
    copies[3].wait()
    copies[4].wait()
    base_ref[: 3 * B, :] = pf_ref[: 3 * B, :] + buf[2] + buf[3]
    base_ref[3 * B :, :] = pf_ref[3 * B :, :]


def own_halves(keep, recv, pf):
    return pl.pallas_call(
        own_kernel,
        out_shape=[jax.ShapeDtypeStruct((3 * B, N), F32), SQUARE],
        in_specs=[FAR] * 3,
        out_specs=[VMEM, VMEM],
        scratch_shapes=[
            pltpu.VMEM((4, 3 * B, N), F32),
            pltpu.VMEM((N, N), F32),
            pltpu.SemaphoreType.DMA((5,)),
        ],
        compiler_params=PARAMS,
        cost_estimate=cost(1),
    )(far(keep), far(recv), far(pf))


def parent_kernel(ids, own_ref, other_ref, x_ref, mine_ref, theirs_ref, out_ref):
    x = split(x_ref[...])
    parity = lax.rem(ids[0], 2)

    @pl.when(parity == 1)
    def _():
        out_ref[...] = dot_split(split(own_ref[...]), x)

    @pl.when(parity == 0)
    def _():
        top = [
            jnp.concatenate(
                [
                    theirs_ref[:, 16 * c : 16 * c + 16, :].reshape(256, B),
                    mine_ref[:, 40 + 16 * c : 56 + 16 * c, :].reshape(256, B),
                ],
                axis=0,
            )
            for c in range(4)
        ]
        top = split(dot_split(split(jnp.concatenate(top, axis=1)), x))
        panel = split(dot_split(split(other_ref[...]), x))
        out_ref[...] = own_ref[...] - dot_split(panel, top)


def parent_step(ids, own, other, x, mine, theirs):
    return pl.pallas_call(
        parent_kernel,
        out_shape=SQUARE,
        in_specs=[SMEM] + [VMEM] * 5,
        out_specs=VMEM,
        compiler_params=PARAMS,
        cost_estimate=cost(4),
    )(ids, own, other, x, mine, theirs)


def fan_tops_kernel(parts_ref, out_ref, sems):
    copies = []
    for t in range(16):
        copies.append(
            pltpu.make_async_copy(parts_ref.at[pl.ds(1, 2)], out_ref.at[t], sems.at[t])
        )
    for copy in copies:
        copy.start()
    for copy in copies:
        copy.wait()


def fan_corner_kernel(parts_ref, out_ref, piece_ref, sems):
    piece_ref[:40, :] = parts_ref[0, :40, :] + parts_ref[1, :40, :]
    piece_ref[40:, :] = parts_ref[1, 40:, :] + parts_ref[2, 40:, :]
    copies = []
    for t in range(16):
        copies.append(pltpu.make_async_copy(piece_ref, out_ref.at[t], sems.at[t]))
    for copy in copies:
        copy.start()
    for copy in copies:
        copy.wait()


def fanned(kernel, parts, shape, scratch):
    return pl.pallas_call(
        kernel,
        out_shape=pltpu.HBM(shape, F32),
        in_specs=[VMEM],
        out_specs=pl.BlockSpec(memory_space=pltpu.HBM),
        scratch_shapes=scratch + [pltpu.SemaphoreType.DMA((16,))],
        compiler_params=PARAMS,
    )(parts)


def exchanged(x):
    return lax.all_to_all(x, "tile", 0, 0)


def gathered(piece):
    return exchanged(jnp.broadcast_to(piece[None], (16,) + piece.shape))


def sibling(x):
    return lax.ppermute(x, "front", [(i, i ^ 1) for i in range(16)])


def local(child_front, parent_front, child_map):
    tile = lax.axis_index("tile")
    front = lax.axis_index("front")
    ids = jnp.stack([front, tile]).astype(jnp.int32)
    parent_vals = parent_front[0]

    pieces = exchanged(spread(ids, child_front))
    pivot = gathered(pieces[0, :80])
    pieces, pivot = lax.optimization_barrier((pieces, pivot))
    fan = fanned(fan_tops_kernel, pieces, (16, 2, B, B), [])
    fan, pivot = lax.optimization_barrier((fan, pivot))
    tops = exchanged(fan).reshape(16, 2 * B, B)
    child_x = inverse_whole(pivot)
    child_panel = panel_of(child_front, child_x)
    keep, send = corner(ids, child_map, child_front, child_panel, tops, child_x, parent_vals)
    summed, panel_later = lax.optimization_barrier((keep + sibling(send), child_panel))
    parts = exchanged(summed)
    keep, send = schur(ids, child_map, child_front, panel_later, child_x, tops)
    send, parts = lax.optimization_barrier((send, parts))
    fan = fanned(fan_corner_kernel, parts, (16, 104, B), [pltpu.VMEM((104, B), F32)])
    mine = exchanged(fan)
    lower, base = own_halves(keep, sibling(send), parent_vals)
    mine, _ = lax.optimization_barrier((mine, lower))
    theirs = sibling(mine[:, :40])
    top_theirs = sibling(mine[:, 40:])
    arrived = lax.ppermute(lower, "tile", [(i, i - 1) for i in range(1, 16)])
    x, s, l = inverse_first(ids, mine, theirs)
    assembled = jnp.concatenate([base[:B], base[B:] + arrived], axis=0)
    assembled, _ = lax.optimization_barrier((assembled, x))
    other = sibling(assembled)
    parent_x = inverse_last(x, s, l)
    result = parent_step(ids, assembled, other, parent_x, mine, top_theirs)
    return (child_panel[None], result[None])


def solution(mesh):
    return jax.shard_map(
        local,
        mesh=mesh,
        in_specs=(P("front", "tile", None), P("front", "tile", None), P()),
        out_specs=(P("front", "tile", None), P("front", "tile", None)),
        check_vma=False,
    )
```

```python
import jax
import jax.numpy as jnp
from jax import lax
from jax.experimental import pallas as pl
from jax.experimental.pallas import tpu as pltpu
from jax.sharding import PartitionSpec as P

B = 128
N = 512
NEAR = 2
NT = ((1,), (1,))
NN = ((1,), (0,))
F32 = jnp.float32
VMEM = pl.BlockSpec(memory_space=pltpu.VMEM)
SMEM = pl.BlockSpec(memory_space=pltpu.SMEM)
PARAMS = pltpu.CompilerParams(vmem_limit_bytes=40 * 1024 * 1024)


def row_of(v, j):
    return jnp.broadcast_to(v[j : j + 1, :], v.shape)


def column_of(v, j):
    return jnp.broadcast_to(v[:, j : j + 1], (v.shape[0], B))


def inverse_factor(rows_at):
    sub = lax.broadcasted_iota(jnp.int32, (8, B), 0)
    lane = lax.broadcasted_iota(jnp.int32, (8, B), 1)
    left = [rows_at(q) for q in range(16)]
    right = [jnp.where(lane == sub + 8 * q, 1.0, 0.0).astype(F32) for q in range(16)]
    out = []
    for p in range(16):
        cols = [column_of(left[p], 8 * p + j) for j in range(8)]
        v, xv = left[p], right[p]
        xf = diag = None
        pivot = row_of(cols[0], 0)
        for j in range(8):
            recip = 1.0 / pivot
            hit = sub == j
            diag = pivot if diag is None else jnp.where(hit, pivot, diag)
            rows = [row_of(cols[m], j) for m in range(j + 1, 8)]
            if j < 7:
                pivot = row_of(cols[j + 1], j + 1) - (rows[0] * rows[0]) * recip
            scale = jnp.where(hit, 0.0, cols[j]) * recip
            for m, cm in zip(range(j + 1, 8), rows):
                cols[m] = jnp.where(hit, cm * recip, cols[m] - scale * cm)
            vr, xr = row_of(v, j), row_of(xv, j)
            xf = xr if xf is None else jnp.where(hit, xr, xf)
            v = jnp.where(hit, vr * recip, v - scale * vr)
            xv = jnp.where(hit, xr * recip, xv - scale * xr)
        out.append(xf * lax.rsqrt(diag))
        near = min(p + NEAR, 15)
        if near < 15:
            rest = jnp.concatenate(left[near + 1 :], axis=0)
            group = lax.broadcasted_iota(jnp.int32, rest.shape, 1) // 8
            rest = split(jnp.where(group == p, rest, 0.0))
            wide = [jnp.concatenate([v, xv], axis=1), jnp.zeros((120 - 8 * p, 2 * B), F32)]
            if p > 0:
                wide = [jnp.zeros((8 * p, 2 * B), F32)] + wide
            both = dot_split(rest, split(jnp.concatenate(wide, axis=0)), NN)
        w = [row_of(v, j) for j in range(8)]
        xw = [row_of(xv, j) for j in range(8)]
        for q in range(p + 1, near + 1):
            c = [column_of(left[q], 8 * p + j) for j in range(8)]
            left[q] = left[q] - total([c[j] * w[j] for j in range(8)])
            right[q] = right[q] - total([c[j] * xw[j] for j in range(8)])
        for q in range(near + 1, 16):
            rows = slice(8 * (q - near - 1), 8 * (q - near))
            left[q] = left[q] - both[rows, :B]
            right[q] = right[q] - both[rows, B:]
    return jnp.concatenate(out, axis=0)


def total(terms):
    while len(terms) > 1:
        terms = [terms[i] + terms[i + 1] for i in range(0, len(terms), 2)]
    return terms[0]


def at(i):
    return pl.ds(pl.multiple_of(i * B, B), B)


LOWER = [(i, j) for i in range(4) for j in range(i + 1)]


def eliminate(steps, s_ref, l_ref, x_ref):
    def step(k, carry):
        k0 = pl.multiple_of(k * B, B)
        xk = inverse_factor(lambda q: s_ref[pl.ds(pl.multiple_of(k0 + 8 * q, 8), 8), at(k)])
        x_ref[at(k), at(k)] = xk
        xs = split(xk)
        for c in range(*steps):

            @pl.when(k == c)
            def _():
                lo, hi = c * B, (c + 1) * B
                if c > 0:
                    w = dot_split(split(l_ref[lo:hi, :lo]), split(x_ref[:lo, :lo]), NN)
                    x_ref[lo:hi, :lo] = -dot_split(xs, split(w), NN)
                if c < 3:
                    col = dot_split(split(s_ref[hi:, lo:hi]), xs)
                    l_ref[hi:, lo:hi] = col
                    col = split(col)
                    s_ref[hi:, hi:] -= dot_split(col, col)

        return carry

    lax.fori_loop(steps[0], steps[1], step, 0)


def unpack(packed, s_ref):
    for b, (i, j) in enumerate(LOWER):
        s_ref[i * B : (i + 1) * B, j * B : (j + 1) * B] = packed[b * B : (b + 1) * B, :]


def whole_kernel(a_ref, out_ref, s_ref, l_ref, x_ref, sem):
    unpack(a_ref[...].reshape(1280, B), s_ref)
    x_ref[...] = jnp.zeros_like(x_ref)
    eliminate((0, 4), s_ref, l_ref, x_ref)
    wait_for(*start_copies([(x_ref, out_ref)], sem))


def first_kernel(ids, mine_ref, theirs_ref, x_ref, s_ref, l_ref, p_ref):
    parity = lax.rem(ids[0], 2)
    p_ref[pl.ds(pl.multiple_of((1 - parity) * 640, 640), 640), :] = mine_ref[:, :40, :].reshape(640, B)
    p_ref[pl.ds(pl.multiple_of(parity * 640, 640), 640), :] = theirs_ref[...].reshape(640, B)
    unpack(p_ref, s_ref)
    x_ref[...] = jnp.zeros_like(x_ref)
    eliminate((0, 3), s_ref, l_ref, x_ref)


def last_kernel(xin_ref, s_ref, l_ref, x_ref):
    x_ref[...] = xin_ref[...]
    eliminate((3, 4), s_ref, l_ref, x_ref)


SQUARE = jax.ShapeDtypeStruct((N, N), F32)
FAR = pl.BlockSpec(memory_space=pltpu.HBM)


PARTS = 4


def start_copies(pairs, sems, first=0):
    groups = []
    for n, (src, dst) in enumerate(pairs):
        step = dst.shape[0] // PARTS
        group = []
        for p in range(PARTS):
            rows = pl.ds(p * step, step)
            sem = sems.at[first + n * PARTS + p]
            group.append(pltpu.make_async_copy(src.at[rows], dst.at[rows], sem))
        groups.append(group)
    for group in groups:
        for copy in group:
            copy.start()
    return groups


def wait_for(*groups):
    for group in groups:
        for copy in group:
            copy.wait()


def far(x):
    return pltpu.with_memory_space_constraint(x, pltpu.HBM)


def cost(gflop):
    return pl.CostEstimate(flops=int(gflop * 1e9), bytes_accessed=2**21, transcendentals=0)


def inverse_whole(packed):
    return pl.pallas_call(
        whole_kernel,
        out_shape=pltpu.HBM((N, N), F32),
        in_specs=[VMEM],
        out_specs=FAR,
        scratch_shapes=[pltpu.VMEM((N, N), F32)] * 3 + [pltpu.SemaphoreType.DMA((PARTS,))],
        compiler_params=PARAMS,
        cost_estimate=cost(25),
    )(packed)


def inverse_first(ids, mine, theirs):
    return pl.pallas_call(
        first_kernel,
        out_shape=[SQUARE] * 3,
        in_specs=[SMEM, VMEM, VMEM],
        out_specs=[VMEM] * 3,
        scratch_shapes=[pltpu.VMEM((1280, B), F32)],
        compiler_params=PARAMS,
        cost_estimate=cost(1),
    )(ids, mine, theirs)


def inverse_last(x, s, l):
    return pl.pallas_call(
        last_kernel,
        out_shape=SQUARE,
        in_specs=[VMEM] * 3,
        out_specs=VMEM,
        compiler_params=PARAMS,
        cost_estimate=cost(6),
    )(x, s, l)


def split(x):
    hi = x.astype(jnp.bfloat16)
    return hi, (x - hi.astype(F32)).astype(jnp.bfloat16)


def dot_split(a, b, dims=NT):
    def dot(u, v):
        return lax.dot_general(u, v, (dims, ((), ())), preferred_element_type=F32)

    return dot(a[0], b[0]) + (dot(a[0], b[1]) + dot(a[1], b[0]))


def symmetric(ref, i, j):
    return 0.5 * (
        ref[i * B : (i + 1) * B, j * B : (j + 1) * B]
        + ref[j * B : (j + 1) * B, i * B : (i + 1) * B].T
    )


def spread_kernel(ids, a_far, out_ref, a_ref, p_ref, sems):
    copies = []
    for c in range(4):
        copy = pltpu.make_async_copy(a_far.at[0, :, pl.ds(c * B, B)], a_ref.at[c], sems.at[c])
        copy.start()
        copies.append(copy)

    def block(i, j):
        return a_ref[j, i * B : (i + 1) * B, :]

    for c, copy in enumerate(copies):
        copy.wait()

        @pl.when(ids[1] > 0)
        def _():
            out_ref[:, 32 * c : 32 * c + 32, :] = a_ref[c].reshape(16, 32, B)

    @pl.when(ids[1] == 0)
    def _():
        for b, (i, j) in enumerate(LOWER):
            p_ref[b * B : (b + 1) * B, :] = 0.5 * (block(i, j) + block(j, i).T)
        out_ref[:, :80, :] = p_ref[...].reshape(16, 80, B)
        out_ref[:, 80:, :] = jnp.zeros((16, 48, B), F32)


def spread(ids, front_vals):
    return pl.pallas_call(
        spread_kernel,
        out_shape=jax.ShapeDtypeStruct((16, B, B), F32),
        in_specs=[SMEM, FAR],
        out_specs=VMEM,
        scratch_shapes=[
            pltpu.VMEM((4, N, B), F32),
            pltpu.VMEM((1280, B), F32),
            pltpu.SemaphoreType.DMA((4,)),
        ],
        compiler_params=PARAMS,
    )(ids, far(front_vals))


def place_of(cmap, front, tile, i):
    return cmap[front, jnp.maximum(4 * tile - 4 + i, 0)] - 4 * (tile - 1)


def panel_kernel(a_far, x_far, out_far, a_ref, x_ref, panel_ref, sems):
    pairs = [(x_far, x_ref), (a_far.at[0, :, pl.ds(0, N)], a_ref)]
    wait_for(*start_copies(pairs, sems))
    panel_ref[...] = dot_split(split(a_ref[...]), split(x_ref[...]))
    wait_for(*start_copies([(panel_ref, out_far)], sems, 2 * PARTS))


def panel_of(front_vals, x):
    return pl.pallas_call(
        panel_kernel,
        out_shape=pltpu.HBM((N, N), F32),
        in_specs=[FAR, FAR],
        out_specs=FAR,
        scratch_shapes=[pltpu.VMEM((N, N), F32)] * 3 + [pltpu.SemaphoreType.DMA((3 * PARTS,))],
        compiler_params=PARAMS,
        cost_estimate=cost(1),
    )(far(front_vals), far(x))


def corner_kernel(
    ids, cmap, a_far, panel_far, top_ref, x_far, pf_far, keep_ref, send_ref,
    a_ref, panel_ref, x_ref, pf_ref, b_ref, p_ref, sems,
):
    copies = start_copies(
        [
            (x_far, x_ref),
            (panel_far, panel_ref),
            (a_far.at[0, :, pl.ds(N, N)], a_ref),
            (pf_far, pf_ref),
        ],
        sems,
    )
    front, tile = ids[0], ids[1]
    parity = lax.rem(front, 2)
    raw = [top_ref[:, 32 * c : 32 * c + 32, :].reshape(N, B) for c in range(4)]
    raw = split(jnp.concatenate(raw, axis=1))
    wait_for(copies[0])
    top = split(dot_split(raw, split(x_ref[...])))
    wait_for(*copies[1:3])
    b_ref[...] = jnp.zeros_like(b_ref)
    for i in range(4):
        rows = slice(i * B, (i + 1) * B)
        first = a_ref[rows, :] - dot_split(split(panel_ref[rows, :]), top)

        @pl.when(tile > 0)
        def _():
            b_ref[at(place_of(cmap, front, tile, i)), :] = first

    wait_for(copies[3])

    @pl.when((tile <= 1) & (parity == 1))
    def _():
        b_ref[pl.ds(pl.multiple_of(tile * N, N), N), :] += pf_ref[...]

    for b, (i, j) in enumerate(LOWER):
        p_ref[b * B : (b + 1) * B, :] = symmetric(b_ref, i, j)
    base = jnp.where(tile == 1, N, 0)
    for ref, half in ((keep_ref, 1 - parity), (send_ref, parity)):
        ref[:, :40, :] = p_ref[pl.ds(pl.multiple_of(half * 640, 640), 640), :].reshape(16, 40, B)
        rows = pl.ds(pl.multiple_of(base + half * 256, 256), 256)
        for c in range(4):
            ref[:, 40 + 16 * c : 56 + 16 * c, :] = b_ref[rows, c * B : (c + 1) * B].reshape(16, 16, B)


def corner(ids, cmap, front_vals, panel, tops, x, pf):
    return pl.pallas_call(
        corner_kernel,
        out_shape=[jax.ShapeDtypeStruct((16, 104, B), F32)] * 2,
        in_specs=[SMEM, SMEM, FAR, FAR, VMEM, FAR, FAR],
        out_specs=[VMEM] * 2,
        scratch_shapes=[pltpu.VMEM((N, N), F32)] * 4
        + [
            pltpu.VMEM((2 * N, N), F32),
            pltpu.VMEM((1280, B), F32),
            pltpu.SemaphoreType.DMA((4 * PARTS,)),
        ],
        compiler_params=PARAMS,
        cost_estimate=cost(3),
    )(ids, cmap, far(front_vals), far(panel), tops, far(x), far(pf))


def schur_kernel(
    ids, cmap, a_far, panel_far, x_far, top_ref, keep_far, out_far,
    a_ref, panel_ref, x_ref, keep_ref, send_ref, ph_ref, pl_ref, sems,
):
    copies = start_copies(
        [(x_far, x_ref), (panel_far, panel_ref), (a_far.at[0, :, pl.ds(N, 2 * N)], a_ref)], sems
    )
    front, tile = ids[0], ids[1]
    parity = lax.rem(front, 2)
    keep_ref[...] = jnp.zeros_like(keep_ref)
    send_ref[...] = jnp.zeros_like(send_ref)
    wait_for(copies[0])
    x = split(x_ref[...])
    out = []
    for h, half, ref, target in (
        (0, parity, send_ref, out_far),
        (1, 1 - parity, keep_ref, keep_far),
    ):
        raw = [
            top_ref[:, pl.ds(pl.multiple_of(half * B + 32 * c, 32), 32), :].reshape(N, B)
            for c in range(4)
        ]
        top = split(dot_split(split(jnp.concatenate(raw, axis=1)), x))
        if h == 0:
            wait_for(*copies[1:])
            ph_ref[...], pl_ref[...] = split(panel_ref[...])
        for i in range(4):
            rows = slice(i * B, (i + 1) * B)
            rest = a_ref[rows, pl.ds(pl.multiple_of(half * N, N), N)]
            rest = rest - dot_split((ph_ref[rows, :], pl_ref[rows, :]), top)

            @pl.when(tile > 0)
            def _():
                ref[at(place_of(cmap, front, tile, i) - 1), :] = rest

        out += start_copies([(ref, target)], sems, (3 + h) * PARTS)
    wait_for(*out)


def schur(ids, cmap, front_vals, panel, x, tops):
    return pl.pallas_call(
        schur_kernel,
        out_shape=[pltpu.HBM((6 * B, N), F32)] * 2,
        in_specs=[SMEM, SMEM, FAR, FAR, FAR, VMEM],
        out_specs=[FAR, FAR],
        scratch_shapes=[
            pltpu.VMEM((N, 2 * N), F32),
            pltpu.VMEM((N, N), F32),
            pltpu.VMEM((N, N), F32),
            pltpu.VMEM((6 * B, N), F32),
            pltpu.VMEM((6 * B, N), F32),
            pltpu.VMEM((N, N), jnp.bfloat16),
            pltpu.VMEM((N, N), jnp.bfloat16),
            pltpu.SemaphoreType.DMA((5 * PARTS,)),
        ],
        compiler_params=PARAMS,
        cost_estimate=cost(8),
    )(ids, cmap, far(front_vals), far(panel), far(x), tops)


def own_kernel(keep_far, recv_far, pf_far, lower_ref, base_ref, buf, pf_ref, sems):
    copies = []
    for h in range(2):
        rows = pl.ds(h * 3 * B, 3 * B)
        for n, ref in enumerate((keep_far, recv_far)):
            copies.append(
                pltpu.make_async_copy(ref.at[rows], buf.at[2 * h + n], sems.at[2 * h + n])
            )
    copies.append(pltpu.make_async_copy(pf_far, pf_ref, sems.at[4]))
    for copy in copies:
        copy.start()
    copies[0].wait()
    copies[1].wait()
    lower_ref[...] = buf[0] + buf[1]
    copies[2].wait()
    copies[3].wait()
    copies[4].wait()
    base_ref[: 3 * B, :] = pf_ref[: 3 * B, :] + buf[2] + buf[3]
    base_ref[3 * B :, :] = pf_ref[3 * B :, :]


def own_halves(keep, recv, pf):
    return pl.pallas_call(
        own_kernel,
        out_shape=[jax.ShapeDtypeStruct((3 * B, N), F32), SQUARE],
        in_specs=[FAR] * 3,
        out_specs=[VMEM, VMEM],
        scratch_shapes=[
            pltpu.VMEM((4, 3 * B, N), F32),
            pltpu.VMEM((N, N), F32),
            pltpu.SemaphoreType.DMA((5,)),
        ],
        compiler_params=PARAMS,
        cost_estimate=cost(1),
    )(far(keep), far(recv), far(pf))


def parent_kernel(ids, own_ref, other_ref, x_ref, mine_ref, theirs_ref, out_ref):
    x = split(x_ref[...])
    parity = lax.rem(ids[0], 2)

    @pl.when(parity == 1)
    def _():
        out_ref[...] = dot_split(split(own_ref[...]), x)

    @pl.when(parity == 0)
    def _():
        top = [
            jnp.concatenate(
                [
                    theirs_ref[:, 16 * c : 16 * c + 16, :].reshape(256, B),
                    mine_ref[:, 40 + 16 * c : 56 + 16 * c, :].reshape(256, B),
                ],
                axis=0,
            )
            for c in range(4)
        ]
        top = split(dot_split(split(jnp.concatenate(top, axis=1)), x))
        panel = split(dot_split(split(other_ref[...]), x))
        out_ref[...] = own_ref[...] - dot_split(panel, top)


def parent_step(ids, own, other, x, mine, theirs):
    return pl.pallas_call(
        parent_kernel,
        out_shape=SQUARE,
        in_specs=[SMEM] + [VMEM] * 5,
        out_specs=VMEM,
        compiler_params=PARAMS,
        cost_estimate=cost(4),
    )(ids, own, other, x, mine, theirs)


def fan_tops_kernel(parts_ref, out_ref, sems):
    copies = []
    for t in range(16):
        copies.append(
            pltpu.make_async_copy(parts_ref.at[pl.ds(1, 2)], out_ref.at[t], sems.at[t])
        )
    for copy in copies:
        copy.start()
    for copy in copies:
        copy.wait()


def fan_corner_kernel(parts_ref, out_ref, piece_ref, sems):
    piece_ref[:40, :] = parts_ref[0, :40, :] + parts_ref[1, :40, :]
    piece_ref[40:, :] = parts_ref[1, 40:, :] + parts_ref[2, 40:, :]
    copies = []
    for t in range(16):
        copies.append(pltpu.make_async_copy(piece_ref, out_ref.at[t], sems.at[t]))
    for copy in copies:
        copy.start()
    for copy in copies:
        copy.wait()


def fanned(kernel, parts, shape, scratch):
    return pl.pallas_call(
        kernel,
        out_shape=pltpu.HBM(shape, F32),
        in_specs=[VMEM],
        out_specs=pl.BlockSpec(memory_space=pltpu.HBM),
        scratch_shapes=scratch + [pltpu.SemaphoreType.DMA((16,))],
        compiler_params=PARAMS,
    )(parts)


def exchanged(x):
    return lax.all_to_all(x, "tile", 0, 0)


def gathered(piece):
    return exchanged(jnp.broadcast_to(piece[None], (16,) + piece.shape))


def sibling(x):
    return lax.ppermute(x, "front", [(i, i ^ 1) for i in range(16)])


def local(child_front, parent_front, child_map):
    tile = lax.axis_index("tile")
    front = lax.axis_index("front")
    ids = jnp.stack([front, tile]).astype(jnp.int32)
    parent_vals = parent_front[0]

    pieces = exchanged(spread(ids, child_front))
    pivot = gathered(pieces[0, :80])
    pieces, pivot = lax.optimization_barrier((pieces, pivot))
    fan = fanned(fan_tops_kernel, pieces, (16, 2, B, B), [])
    fan, pivot = lax.optimization_barrier((fan, pivot))
    tops = exchanged(fan).reshape(16, 2 * B, B)
    child_x = inverse_whole(pivot)
    child_panel = panel_of(child_front, child_x)
    keep, send = corner(ids, child_map, child_front, child_panel, tops, child_x, parent_vals)
    summed, panel_later = lax.optimization_barrier((keep + sibling(send), child_panel))
    parts = exchanged(summed)
    keep, send = schur(ids, child_map, child_front, panel_later, child_x, tops)
    send, parts = lax.optimization_barrier((send, parts))
    fan = fanned(fan_corner_kernel, parts, (16, 104, B), [pltpu.VMEM((104, B), F32)])
    mine = exchanged(fan)
    lower, base = own_halves(keep, sibling(send), parent_vals)
    mine, _ = lax.optimization_barrier((mine, lower))
    theirs = sibling(mine[:, :40])
    top_theirs = sibling(mine[:, 40:])
    arrived = lax.ppermute(lower, "tile", [(i, i - 1) for i in range(1, 16)])
    x, s, l = inverse_first(ids, mine, theirs)
    assembled = jnp.concatenate([base[:B], base[B:] + arrived], axis=0)
    assembled, _ = lax.optimization_barrier((assembled, x))
    other = sibling(assembled)
    parent_x = inverse_last(x, s, l)
    result = parent_step(ids, assembled, other, parent_x, mine, top_theirs)
    return (child_panel[None], result[None])


def solution(mesh):
    return jax.shard_map(
        local,
        mesh=mesh,
        in_specs=(P("front", "tile", None), P("front", "tile", None), P()),
        out_specs=(P("front", "tile", None), P("front", "tile", None)),
        check_vma=False,
    )
```
